32 devices in a mesh: scen: 4 (over y, x), row: 4 (over z), col: 2 (over core).
Axes of the slice: x: 2, y: 2, z: 4, core: 2. Of those that a mesh axis runs over, the one named last changes fastest.
Arguments:
- border: bfloat16 [16, 4, 512, 512], P('scen', None, ('row', 'col')), may hold values from -4.5 to 4.5, as said below
- panel_border: bfloat16 [16, 512, 512], P('scen'), may hold values from -0.26516504 to 0.26516504
- kinv: bfloat16 [16, 512, 512], P('scen'), may hold values from -1 to 4, as said below
- factor: bfloat16 [2048, 4096], P(('scen', 'row'), 'col'), may hold values from -4.5 to 4.5
- root_block: float32 [2048, 512], P(('scen', 'row', 'col')), may hold values from -9 to 43, as said below
Outputs:
- panel_factor: float32 [2048, 512], P(('scen', 'row', 'col'))
The draws below stay inside these ranges and needn't reach their ends.
Inputs may be any that keep to these rules, and one draw needn't show every extreme that they name: border[s, 0] is panel_border[s] transposed. `kinv`: each scenario's matrix is symmetric positive definite up to rounding, with eigenvalues 0.5 or more. `root_block`: its first 512 rows form a symmetric matrix; schur[0:512] is positive definite.
All inputs are finite; a program needn't handle non-finite values.
Results may differ from the reference program's by a relative error of at most 0.0025.
Values may be sent and summed in bfloat16 or wider, within the bound.
A program may use at most 128 MiB of HBM per device.

```python
import jax
import jax.numpy as jnp
from jax import lax

NS = 512
PANEL = 512
KRES = 4096
SCEN = 16
ROWS = 2048
N_SCEN = 4


def panel_columns(key):
    base = jnp.clip(jax.random.normal(jax.random.fold_in(key, 7), (SCEN, NS, PANEL), jnp.float32), -6.0, 6.0)
    return base * (SCEN * NS / 16.0) ** (-0.5)


def draw_panel_border(key, part):
    return panel_columns(key).astype(jnp.bfloat16)


def draw_border(key, part):
    base = jnp.clip(jax.random.normal(jax.random.fold_in(key, 11), (SCEN, N_SCEN, PANEL, NS), jnp.float32), -6.0, 6.0) * 0.75
    own = jnp.transpose(panel_columns(key), (0, 2, 1))
    return base.at[:, 0].set(own).astype(jnp.bfloat16)


def draw_kinv(key, part):
    base = jax.random.normal(key, (SCEN, NS, NS), jnp.float32)
    gram = jnp.einsum('snk,smk->snm', base, base, precision=lax.Precision.HIGHEST) / (2.0 * NS)
    return (gram + 0.5 * jnp.eye(NS, dtype=jnp.float32)).astype(jnp.bfloat16)


def draw_factor(key, part):
    base = jnp.clip(jax.random.normal(key, (ROWS, KRES), jnp.float32), -6.0, 6.0)
    places = lax.broadcasted_iota(jnp.int32, (ROWS, 1), 0)
    scales = jnp.where(places < PANEL, 2.0 / KRES ** 0.5, 0.75)
    return (base * scales).astype(jnp.bfloat16)


def draw_root_block(key, part):
    base = jnp.clip(jax.random.normal(key, (ROWS, PANEL), jnp.float32), -6.0, 6.0)
    square = base[0:PANEL]
    block = (square + square.T) * 0.212 + 40.0 * jnp.eye(PANEL, dtype=jnp.float32)
    return jnp.concatenate([block, 1.5 * base[PANEL:]], axis=0)


def setup_inputs(seed: int = 0) -> dict:
    splits = jax.random.split(jax.random.key(seed), 6)
    border = draw_border(jax.random.fold_in(splits[5], 71), 0)
    panel_border = draw_panel_border(jax.random.fold_in(splits[5], 71), 0)
    kinv = draw_kinv(jax.random.fold_in(splits[5], 71), 0)
    factor = draw_factor(jax.random.fold_in(splits[5], 71), 0)
    root_block = draw_root_block(jax.random.fold_in(splits[5], 71), 0)
    return dict(border=border, panel_border=panel_border, kinv=kinv, factor=factor, root_block=root_block)


def reference(border, panel_border, kinv, factor, root_block):
    slab = border.reshape(SCEN, ROWS, NS)

    def add_scenario(total, items):
        rows_part, panel_part, inverse = items
        solved = jnp.dot(inverse.astype(jnp.float32), panel_part.astype(jnp.float32), preferred_element_type=jnp.float32).astype(jnp.bfloat16)
        return (total + jnp.dot(rows_part.astype(jnp.float32), solved.astype(jnp.float32), preferred_element_type=jnp.float32), None)
    coupling, unused = lax.scan(add_scenario, jnp.zeros((ROWS, PANEL), jnp.float32), (slab, panel_border, kinv))
    leading = factor[0:PANEL]
    update = lax.dot_general(factor.astype(jnp.float32), leading.astype(jnp.float32), (((1,), (1,)), ((), ())), preferred_element_type=jnp.float32)
    schur = root_block + coupling - update
    lower = jnp.linalg.cholesky(schur[0:PANEL])
    return jax.scipy.linalg.solve_triangular(lower, schur.T, lower=True).T
```

```python
import functools

import jax
import jax.numpy as jnp
from jax import lax
from jax.experimental import pallas as pl
from jax.experimental.pallas import tpu as pltpu
from jax.sharding import PartitionSpec as P

MESH = pl.DeviceIdType.MESH
F32 = jnp.float32
BLOCK = 128
STRIP = 16
HIGHEST = lax.Precision.HIGHEST


def mm(a, b, da, db, precision=None):
    return lax.dot_general(
        a, b, (((da,), (db,)), ((), ())), precision=precision, preferred_element_type=F32
    )


def gather_kernel(
    S, R, C,
    border_ref, pb_ref, kinv_ref, factor_ref, root_ref,
    schur_ref, diag_ref,
    lead, roots, solved, cp, rs_a, dp, rs_b, dall, upd, upd_in, part_in,
    tree_send, tree_recv, line_send, line_recv,
    a_send, a_recv, b_send, b_recv, g_send, g_recv,
    u_send, u_recv, p_send, p_recv, local_sem,
):
    s, r, c = lax.axis_index("scen"), lax.axis_index("row"), lax.axis_index("col")
    bits = S.bit_length() - 1
    chunks = tree_send.shape[0] - 1
    rows = factor_ref.shape[0]
    own = root_ref.shape[0]
    panel = root_ref.shape[1]
    step = rows // chunks
    half = panel // C
    n = half // S

    def peer_s(o):
        return lax.rem(s + o, S)

    def peer_r(o):
        return lax.rem(r + o, R)

    barrier = pltpu.get_barrier_semaphore()
    for o in range(1, S):
        pl.semaphore_signal(barrier, inc=1, device_id=(peer_s(o), r, c), device_id_type=MESH)
    for o in range(1, R):
        pl.semaphore_signal(barrier, inc=1, device_id=(s, peer_r(o), c), device_id_type=MESH)
    pl.semaphore_signal(barrier, inc=1, device_id=(s, r, 1 - c), device_id_type=MESH)
    pl.semaphore_wait(barrier, S + R - 1)

    def piece(k):
        if k == chunks:
            return roots.at[r]
        return lead.at[pl.ds(pl.multiple_of(r * rows + k * step, step), step), :]

    def tree_copy(k, j, up):
        ref = piece(k)
        return pltpu.make_async_remote_copy(
            src_ref=ref, dst_ref=ref, send_sem=tree_send.at[k, j], recv_sem=tree_recv.at[k],
            device_id=(up, r, c), device_id_type=MESH,
        )

    def tree_cond(k, j):
        bit = 1 << j
        if k % 2 == 0:
            return s < bit
        return lax.rem(s, 2 * bit) == 0

    def line_copy(k, o):
        ref = piece(k)
        return pltpu.make_async_remote_copy(
            src_ref=ref, dst_ref=ref, send_sem=line_send.at[k, o - 1], recv_sem=line_recv.at[k, o - 1],
            device_id=(s, peer_r(o), c), device_id_type=MESH,
        )

    order = list(range(chunks)) + [chunks]

    @pl.when(s == 0)
    def _():
        lead[pl.ds(pl.multiple_of(r * rows, rows), rows), :] = factor_ref[...]
        roots[r] = root_ref[...]

    def pass_on(k):
        @pl.when(s != 0)
        def _():
            tree_copy(k, 0, s).wait_recv()

        for j in range(bits):
            @pl.when(tree_cond(k, j))
            def _():
                tree_copy(k, j, lax.rem(s + (1 << j), S)).start()
        for o in range(1, R):
            line_copy(k, o).start()

    def a_copy(o):
        return pltpu.make_async_remote_copy(
            src_ref=cp.at[peer_s(o)], dst_ref=rs_a.at[o - 1], send_sem=a_send.at[o - 1],
            recv_sem=a_recv.at[o - 1], device_id=(peer_s(o), r, c), device_id_type=MESH,
        )

    def b_copy(o):
        return pltpu.make_async_remote_copy(
            src_ref=dp.at[pl.ds(pl.multiple_of(peer_s(o) * n, n), n), :], dst_ref=rs_b.at[o - 1],
            send_sem=b_send.at[o - 1], recv_sem=b_recv.at[o - 1],
            device_id=(peer_s(o), r, c), device_id_type=MESH,
        )

    def g_copy(o):
        ref = dall.at[pl.ds(pl.multiple_of(s * n, n), n), :]
        return pltpu.make_async_remote_copy(
            src_ref=ref, dst_ref=ref, send_sem=g_send.at[o - 1], recv_sem=g_recv.at[o - 1],
            device_id=(peer_s(o), r, c), device_id_type=MESH,
        )

    @pl.when(s == 0)
    def _():
        for k in order:
            pass_on(k)

    scenarios = kinv_ref.shape[0]
    dp[...] = jnp.zeros_like(dp)
    cp[...] = jnp.zeros_like(cp)
    groups = cp.shape[0]

    @pl.loop(0, scenarios)
    def _(i):
        sol = mm(kinv_ref[i], pb_ref[i], 1, 0).astype(jnp.bfloat16)
        solved[i] = sol
        cols = pb_ref[i, :, pl.ds(pl.multiple_of(c * half, half), half)]
        dp[...] += mm(cols, sol, 0, 0)

    for o in range(1, S):
        b_copy(o).start()

    @pl.loop(0, scenarios)
    def _(i):
        @pl.loop(0, groups)
        def _(g):
            cp[g] += mm(border_ref[i, g], solved[i], 1, 0)

    @pl.when(s != 0)
    def _():
        for k in order:
            pass_on(k)

    for o in range(1, S):
        a_copy(o).start()
    mine = pl.ds(pl.multiple_of(s * n, n), n)
    total = dp[mine, :]
    for o in range(1, S):
        b_copy(o).wait_recv()
        total += rs_b[o - 1]
    dall[mine, :] = total
    for o in range(1, S):
        g_copy(o).start()

    for k in order:
        for o in range(1, R):
            line_copy(k, o).wait_recv()
    for o in range(1, S):
        g_copy(o).wait_recv()

    def p_copy(q):
        at = pl.ds(q * rows, rows)
        return pltpu.make_async_remote_copy(
            src_ref=diag_ref.at[at, :], dst_ref=part_in.at[at, :], send_sem=p_send.at[q],
            recv_sem=p_recv.at[q], device_id=(s, r, 1 - c), device_id_type=MESH,
        )

    diag_ref[...] = -mm(lead[...], lead[...], 1, 1)
    there = pl.ds(pl.multiple_of(c * half, half), half)
    diag_ref[there, :] += dall[...]
    for q in range(R):
        at = pl.ds(pl.multiple_of((q * C + c) * own, own), own)
        diag_ref[at, :] += roots[q]
    for q in range(R):
        p_copy(q).start()

    u_copy = pltpu.make_async_remote_copy(
        src_ref=upd.at[1 - c], dst_ref=upd_in, send_sem=u_send, recv_sem=u_recv,
        device_id=(s, r, 1 - c), device_id_type=MESH,
    )
    product = mm(factor_ref[...], lead[...], 1, 1)
    for q in range(C):
        upd[q] = product[q * own:(q + 1) * own]
    u_copy.start()

    acc = root_ref[...] + cp[s] - upd[c]
    for o in range(1, S):
        a_copy(o).wait_recv()
        acc += rs_a[o - 1]
    u_copy.wait()
    schur_ref[...] = acc - upd_in[...]
    for q in range(R):
        p_copy(q).wait()
    diag_ref[...] += part_in[...]

    for k in order:
        for j in range(bits):
            @pl.when(tree_cond(k, j))
            def _():
                tree_copy(k, j, lax.rem(s + (1 << j), S)).wait_send()
        for o in range(1, R):
            line_copy(k, o).wait_send()
    for o in range(1, S):
        a_copy(o).wait_send()
        b_copy(o).wait_send()
        g_copy(o).wait_send()


def gather(S, R, C, border, panel_border, kinv, factor, root):
    rows, depth = factor.shape
    own, panel = root.shape
    groups = border.shape[1]
    half = panel // C
    n = half // S
    bits = S.bit_length() - 1
    chunks = 4
    dma = pltpu.SemaphoreType.DMA
    vmem = pl.BlockSpec(memory_space=pltpu.VMEM)
    return pl.pallas_call(
        functools.partial(gather_kernel, S, R, C),
        out_shape=(
            jax.ShapeDtypeStruct((own, panel), F32),
            jax.ShapeDtypeStruct((panel, panel), F32),
        ),
        in_specs=[vmem] * 5,
        out_specs=(vmem, vmem),
        scratch_shapes=[
            pltpu.VMEM((R * rows, depth), jnp.bfloat16),
            pltpu.VMEM((R, own, panel), F32),
            pltpu.VMEM(kinv.shape, jnp.bfloat16),
            pltpu.VMEM((groups, own, panel), F32),
            pltpu.VMEM((S - 1, own, panel), F32),
            pltpu.VMEM((half, panel), F32),
            pltpu.VMEM((S - 1, n, panel), F32),
            pltpu.VMEM((half, panel), F32),
            pltpu.VMEM((C, own, panel), F32),
            pltpu.VMEM((own, panel), F32),
            pltpu.VMEM((panel, panel), F32),
            dma((chunks + 1, bits)),
            dma((chunks + 1,)),
            dma((chunks + 1, R - 1)),
            dma((chunks + 1, R - 1)),
            dma((S - 1,)), dma((S - 1,)), dma((S - 1,)), dma((S - 1,)), dma((S - 1,)), dma((S - 1,)),
            dma, dma, dma((R,)), dma((R,)), dma,
        ],
        compiler_params=pltpu.CompilerParams(
            collective_id=0, has_side_effects=True, vmem_limit_bytes=56 * 1024 * 1024
        ),
    )(border, panel_border, kinv, factor, root)


def factor_block(work):
    size = work.shape[0]
    sub = lax.broadcasted_iota(jnp.int32, (STRIP, BLOCK), 0)
    for j in range(size // STRIP):
        lo = j * STRIP
        left = work[lo:lo + STRIP, 0:BLOCK]
        right = work[lo:lo + STRIP, BLOCK:2 * BLOCK]
        cols = [
            jnp.broadcast_to(left[:, lo + b:lo + b + 1], (STRIP, BLOCK)) for b in range(STRIP)
        ]
        scale = jnp.zeros((STRIP, BLOCK), F32)
        for k in range(STRIP):
            pivot = jnp.broadcast_to(cols[k][k:k + 1, :], (STRIP, BLOCK))
            inverse = pl.reciprocal(pivot, approx=True)
            inverse = inverse * (2.0 - pivot * inverse)
            scale = jnp.where(sub == k, lax.rsqrt(pivot), scale)
            if k + 1 < STRIP:
                times = jnp.where(sub > k, cols[k] * inverse, 0.0)
                for b in range(k + 1, STRIP):
                    cols[b] = cols[b] - times * cols[b][k:k + 1, :]
                left = left - times * left[k:k + 1, :]
                right = right - times * right[k:k + 1, :]
        left = left * scale
        right = right * scale
        work[lo:lo + STRIP, 0:BLOCK] = left
        work[lo:lo + STRIP, BLOCK:2 * BLOCK] = right
        if lo + STRIP < size:
            both = jnp.concatenate([left, right], axis=1)
            work[lo + STRIP:, :] -= mm(left, both, 0, 0, HIGHEST)[lo + STRIP:, :]


def cholesky_kernel(schur_ref, diag_ref, out_ref, aug, work):
    own, panel = schur_ref.shape
    blocks = panel // BLOCK
    down = lax.broadcasted_iota(jnp.int32, (BLOCK, BLOCK), 0)
    across = lax.broadcasted_iota(jnp.int32, (BLOCK, BLOCK), 1)
    eye = jnp.where(down == across, 1.0, 0.0).astype(F32)
    aug[:, 0:panel] = diag_ref[...].T
    aug[:, panel:panel + own] = schur_ref[...].T

    @pl.loop(0, blocks)
    def _(J):
        at = pl.ds(pl.multiple_of(J * BLOCK, BLOCK), BLOCK)
        square = aug[at, at]
        work[:, 0:BLOCK] = jnp.where(down <= across, square, square.T)
        work[:, BLOCK:2 * BLOCK] = eye
        factor_block(work)
        rows = mm(work[:, BLOCK:2 * BLOCK], aug[at, :], 1, 0, HIGHEST)
        aug[at, :] = rows

        @pl.loop(J + 1, blocks)
        def _(i):
            it = pl.ds(pl.multiple_of(i * BLOCK, BLOCK), BLOCK)
            aug[it, :] -= mm(aug[at, it], aug[at, :], 0, 0, HIGHEST)

    out_ref[...] = aug[:, panel:panel + own].T


def finish(schur, diag):
    own, panel = schur.shape
    vmem = pl.BlockSpec(memory_space=pltpu.VMEM)
    return pl.pallas_call(
        cholesky_kernel,
        out_shape=jax.ShapeDtypeStruct(schur.shape, F32),
        in_specs=[vmem, vmem],
        out_specs=vmem,
        scratch_shapes=[
            pltpu.VMEM((panel, panel + own), F32),
            pltpu.VMEM((BLOCK, 2 * BLOCK), F32),
        ],
        compiler_params=pltpu.CompilerParams(vmem_limit_bytes=32 * 1024 * 1024),
    )(schur, diag)


def solution(mesh):
    S, R, C = mesh.shape["scen"], mesh.shape["row"], mesh.shape["col"]
    in_specs = (
        P("scen", None, ("row", "col"), None),
        P("scen", None, None),
        P("scen", None, None),
        P(("scen", "row"), "col"),
        P(("scen", "row", "col"), None),
    )
    out_specs = P(("scen", "row", "col"), None)

    def per_device(border, panel_border, kinv, factor, root_block):
        schur, diag = gather(S, R, C, border, panel_border, kinv, factor, root_block)
        return finish(schur, diag)

    return jax.shard_map(
        per_device, mesh=mesh, in_specs=in_specs, out_specs=out_specs, check_vma=False
    )
```

```python
import functools

import jax
import jax.numpy as jnp
from jax import lax
from jax.experimental import pallas as pl
from jax.experimental.pallas import tpu as pltpu
from jax.sharding import PartitionSpec as P

MESH = pl.DeviceIdType.MESH
F32 = jnp.float32
BLOCK = 128
STRIP = 16
HIGHEST = lax.Precision.HIGHEST


def mm(a, b, da, db, precision=None):
    return lax.dot_general(
        a, b, (((da,), (db,)), ((), ())), precision=precision, preferred_element_type=F32
    )


def gather_kernel(
    S, R, C,
    border_ref, pb_ref, kinv_ref, factor_ref, root_ref,
    schur_ref, diag_ref,
    lead, roots, solved, full, cp, rs_a, dp, rs_b, dall, upd, upd_in, part_in,
    tree_send, tree_recv, line_send, line_recv,
    a_send, a_recv, b_send, b_recv, g_send, g_recv,
    u_send, u_recv, p_send, p_recv,
):
    s, r, c = lax.axis_index("scen"), lax.axis_index("row"), lax.axis_index("col")
    bits = S.bit_length() - 1
    chunks = tree_send.shape[0]
    rows = factor_ref.shape[0]
    own = root_ref.shape[0]
    panel = root_ref.shape[1]
    step = rows // chunks
    half = panel // C
    n = half // S

    def peer_s(o):
        return lax.rem(s + o, S)

    def peer_r(o):
        return lax.rem(r + o, R)

    barrier = pltpu.get_barrier_semaphore()
    for o in range(1, S):
        pl.semaphore_signal(barrier, inc=1, device_id=(peer_s(o), r, c), device_id_type=MESH)
    for o in range(1, R):
        pl.semaphore_signal(barrier, inc=1, device_id=(s, peer_r(o), c), device_id_type=MESH)
    pl.semaphore_signal(barrier, inc=1, device_id=(s, r, 1 - c), device_id_type=MESH)
    pl.semaphore_wait(barrier, S + R - 1)

    def piece(q, k):
        if k == chunks:
            return roots.at[q]
        return lead.at[pl.ds(pl.multiple_of(q * rows + k * step, step), step), :]

    def tree_copy(k, j, up):
        ref = piece(r, k)
        return pltpu.make_async_remote_copy(
            src_ref=ref, dst_ref=ref, send_sem=tree_send.at[k, j], recv_sem=tree_recv.at[k],
            device_id=(up, r, c), device_id_type=MESH,
        )

    def tree_cond(k, j):
        bit = 1 << j
        if k % 2 == 0:
            return s < bit
        return lax.rem(s, 2 * bit) == 0

    def line_copy(q, k, up):
        ref = piece(q, k)
        return pltpu.make_async_remote_copy(
            src_ref=ref, dst_ref=ref, send_sem=line_send.at[k, q, 1 if up else 0],
            recv_sem=line_recv.at[k, q],
            device_id=(s, lax.rem(r + (1 if up else R - 1), R), c), device_id_type=MESH,
        )

    def line_start(q, k, up):
        @pl.when(r < R - 1 if up else r > 0)
        def _():
            line_copy(q, k, up).start()

    def hop(d, k):
        @pl.when(r >= d)
        def _():
            line_copy(r - d, k, True).wait_recv()
            line_start(r - d, k, True)

        @pl.when(r + d < R)
        def _():
            line_copy(r + d, k, False).wait_recv()
            line_start(r + d, k, False)

    def line_sent(k):
        @pl.when(r < R - 1)
        def _():
            for d in range(R):
                @pl.when(r >= d)
                def _():
                    line_copy(r - d, k, True).wait_send()

        @pl.when(r > 0)
        def _():
            for d in range(R):
                @pl.when(r + d < R)
                def _():
                    line_copy(r + d, k, False).wait_send()

    def pass_on(k):
        @pl.when(s != 0)
        def _():
            tree_copy(k, 0, s).wait_recv()

        for j in range(bits):
            @pl.when(tree_cond(k, j))
            def _():
                tree_copy(k, j, lax.rem(s + (1 << j), S)).start()
        line_start(r, k, True)
        line_start(r, k, False)

    def a_copy(o):
        return pltpu.make_async_remote_copy(
            src_ref=cp.at[peer_s(o)], dst_ref=rs_a.at[o - 1], send_sem=a_send.at[o - 1],
            recv_sem=a_recv.at[o - 1], device_id=(peer_s(o), r, c), device_id_type=MESH,
        )

    def b_copy(o):
        return pltpu.make_async_remote_copy(
            src_ref=dp.at[pl.ds(pl.multiple_of(peer_s(o) * n, n), n), :], dst_ref=rs_b.at[o - 1],
            send_sem=b_send.at[o - 1], recv_sem=b_recv.at[o - 1],
            device_id=(peer_s(o), r, c), device_id_type=MESH,
        )

    def g_copy(o):
        ref = dall.at[pl.ds(pl.multiple_of(s * n, n), n), :]
        return pltpu.make_async_remote_copy(
            src_ref=ref, dst_ref=ref, send_sem=g_send.at[o - 1], recv_sem=g_recv.at[o - 1],
            device_id=(peer_s(o), r, c), device_id_type=MESH,
        )

    @pl.when(s == 0)
    def _():
        lead[pl.ds(pl.multiple_of(r * rows, rows), rows), :] = factor_ref[...]
        roots[r] = root_ref[...]
        line_start(r, chunks, True)
        line_start(r, chunks, False)
        for k in range(chunks):
            pass_on(k)

    scenarios = kinv_ref.shape[0]
    full[...] = jnp.zeros_like(full)
    cp[...] = jnp.zeros_like(cp)
    groups = cp.shape[0]

    @pl.loop(0, scenarios)
    def _(i):
        sol = mm(kinv_ref[i], pb_ref[i], 1, 0).astype(jnp.bfloat16)
        solved[i] = sol
        full[...] += mm(pb_ref[i], sol, 0, 0)

    for q in range(R):
        dp[q * own:(q + 1) * own, :] = full[pl.ds(pl.multiple_of((q * C + c) * own, own), own), :]

    @pl.when(s == 0)
    def _():
        for d in range(1, R):
            hop(d, chunks)
        for q in range(R):
            dp[q * own:(q + 1) * own, :] += roots[q]

    for o in range(1, S):
        b_copy(o).start()

    @pl.loop(0, scenarios)
    def _(i):
        @pl.loop(0, groups)
        def _(g):
            cp[g] += mm(border_ref[i, g], solved[i], 1, 0)

    mine = pl.ds(pl.multiple_of(s * n, n), n)
    for t in range(chunks + R - 1):
        if t < chunks:
            @pl.when(s != 0)
            def _():
                pass_on(t)
        if t == chunks - 1:
            for o in range(1, S):
                a_copy(o).start()
            total = dp[mine, :]
            for o in range(1, S):
                b_copy(o).wait_recv()
                total += rs_b[o - 1]
            dall[mine, :] = total
            for o in range(1, S):
                g_copy(o).start()
        for d in range(1, R):
            if 0 <= t - d < chunks:
                hop(d, t - d)
    for o in range(1, S):
        g_copy(o).wait_recv()

    def p_copy(q):
        at = pl.ds(q * rows, rows)
        return pltpu.make_async_remote_copy(
            src_ref=diag_ref.at[at, :], dst_ref=part_in.at[at, :], send_sem=p_send.at[q],
            recv_sem=p_recv.at[q], device_id=(s, r, 1 - c), device_id_type=MESH,
        )

    diag_ref[...] = -mm(lead[...], lead[...], 1, 1)
    for q in range(R):
        at = pl.ds(pl.multiple_of((q * C + c) * own, own), own)
        diag_ref[at, :] += dall[q * own:(q + 1) * own, :]
    for q in range(R):
        p_copy(q).start()

    u_copy = pltpu.make_async_remote_copy(
        src_ref=upd.at[1 - c], dst_ref=upd_in, send_sem=u_send, recv_sem=u_recv,
        device_id=(s, r, 1 - c), device_id_type=MESH,
    )
    product = mm(factor_ref[...], lead[...], 1, 1)
    for q in range(C):
        upd[q] = product[q * own:(q + 1) * own]
    u_copy.start()

    acc = root_ref[...] + cp[s] - upd[c]
    for o in range(1, S):
        a_copy(o).wait_recv()
        acc += rs_a[o - 1]
    u_copy.wait()
    schur_ref[...] = acc - upd_in[...]
    for q in range(R):
        p_copy(q).wait()
    diag_ref[...] += part_in[...]

    for k in range(chunks):
        for j in range(bits):
            @pl.when(tree_cond(k, j))
            def _():
                tree_copy(k, j, lax.rem(s + (1 << j), S)).wait_send()
        line_sent(k)

    @pl.when(s == 0)
    def _():
        line_sent(chunks)

    for o in range(1, S):
        a_copy(o).wait_send()
        b_copy(o).wait_send()
        g_copy(o).wait_send()


def gather(S, R, C, border, panel_border, kinv, factor, root):
    rows, depth = factor.shape
    own, panel = root.shape
    groups = border.shape[1]
    half = panel // C
    n = half // S
    bits = S.bit_length() - 1
    chunks = 4
    dma = pltpu.SemaphoreType.DMA
    vmem = pl.BlockSpec(memory_space=pltpu.VMEM)
    return pl.pallas_call(
        functools.partial(gather_kernel, S, R, C),
        out_shape=(
            jax.ShapeDtypeStruct((own, panel), F32),
            jax.ShapeDtypeStruct((panel, panel), F32),
        ),
        in_specs=[vmem] * 5,
        out_specs=(vmem, vmem),
        scratch_shapes=[
            pltpu.VMEM((R * rows, depth), jnp.bfloat16),
            pltpu.VMEM((R, own, panel), F32),
            pltpu.VMEM(kinv.shape, jnp.bfloat16),
            pltpu.VMEM((panel, panel), F32),
            pltpu.VMEM((groups, own, panel), F32),
            pltpu.VMEM((S - 1, own, panel), F32),
            pltpu.VMEM((half, panel), F32),
            pltpu.VMEM((S - 1, n, panel), F32),
            pltpu.VMEM((half, panel), F32),
            pltpu.VMEM((C, own, panel), F32),
            pltpu.VMEM((own, panel), F32),
            pltpu.VMEM((panel, panel), F32),
            dma((chunks, bits)),
            dma((chunks,)),
            dma((chunks + 1, R, 2)),
            dma((chunks + 1, R)),
            dma((S - 1,)), dma((S - 1,)), dma((S - 1,)), dma((S - 1,)), dma((S - 1,)), dma((S - 1,)),
            dma, dma, dma((R,)), dma((R,)),
        ],
        compiler_params=pltpu.CompilerParams(
            collective_id=0, has_side_effects=True, vmem_limit_bytes=56 * 1024 * 1024
        ),
    )(border, panel_border, kinv, factor, root)


def factor_block(work):
    size = work.shape[0]
    sub = lax.broadcasted_iota(jnp.int32, (STRIP, BLOCK), 0)
    for j in range(size // STRIP):
        lo = j * STRIP
        left = work[lo:lo + STRIP, 0:BLOCK]
        right = work[lo:lo + STRIP, BLOCK:2 * BLOCK]
        cols = [
            jnp.broadcast_to(left[:, lo + b:lo + b + 1], (STRIP, BLOCK)) for b in range(STRIP)
        ]
        scale = jnp.zeros((STRIP, BLOCK), F32)
        for k in range(STRIP):
            pivot = jnp.broadcast_to(cols[k][k:k + 1, :], (STRIP, BLOCK))
            inverse = pl.reciprocal(pivot, approx=True)
            inverse = inverse * (2.0 - pivot * inverse)
            scale = jnp.where(sub == k, lax.rsqrt(pivot), scale)
            if k + 1 < STRIP:
                times = jnp.where(sub > k, cols[k] * inverse, 0.0)
                for b in range(k + 1, STRIP):
                    cols[b] = cols[b] - times * cols[b][k:k + 1, :]
                left = left - times * left[k:k + 1, :]
                right = right - times * right[k:k + 1, :]
        left = left * scale
        right = right * scale
        work[lo:lo + STRIP, 0:BLOCK] = left
        work[lo:lo + STRIP, BLOCK:2 * BLOCK] = right
        if lo + STRIP < size:
            both = jnp.concatenate([left, right], axis=1)
            work[lo + STRIP:, :] -= mm(left, both, 0, 0, HIGHEST)[lo + STRIP:, :]


def cholesky_kernel(schur_ref, diag_ref, out_ref, aug, work):
    own, panel = schur_ref.shape
    blocks = panel // BLOCK
    down = lax.broadcasted_iota(jnp.int32, (BLOCK, BLOCK), 0)
    across = lax.broadcasted_iota(jnp.int32, (BLOCK, BLOCK), 1)
    eye = jnp.where(down == across, 1.0, 0.0).astype(F32)
    aug[:, 0:panel] = diag_ref[...].T
    aug[:, panel:panel + own] = schur_ref[...].T

    @pl.loop(0, blocks)
    def _(J):
        at = pl.ds(pl.multiple_of(J * BLOCK, BLOCK), BLOCK)
        square = aug[at, at]
        work[:, 0:BLOCK] = jnp.where(down <= across, square, square.T)
        work[:, BLOCK:2 * BLOCK] = eye
        factor_block(work)
        rows = mm(work[:, BLOCK:2 * BLOCK], aug[at, :], 1, 0, HIGHEST)
        aug[at, :] = rows

        @pl.loop(J + 1, blocks)
        def _(i):
            it = pl.ds(pl.multiple_of(i * BLOCK, BLOCK), BLOCK)
            aug[it, :] -= mm(aug[at, it], aug[at, :], 0, 0, HIGHEST)

    out_ref[...] = aug[:, panel:panel + own].T


def finish(schur, diag):
    own, panel = schur.shape
    vmem = pl.BlockSpec(memory_space=pltpu.VMEM)
    return pl.pallas_call(
        cholesky_kernel,
        out_shape=jax.ShapeDtypeStruct(schur.shape, F32),
        in_specs=[vmem, vmem],
        out_specs=vmem,
        scratch_shapes=[
            pltpu.VMEM((panel, panel + own), F32),
            pltpu.VMEM((BLOCK, 2 * BLOCK), F32),
        ],
        compiler_params=pltpu.CompilerParams(vmem_limit_bytes=32 * 1024 * 1024),
    )(schur, diag)


def solution(mesh):
    S, R, C = mesh.shape["scen"], mesh.shape["row"], mesh.shape["col"]
    in_specs = (
        P("scen", None, ("row", "col"), None),
        P("scen", None, None),
        P("scen", None, None),
        P(("scen", "row"), "col"),
        P(("scen", "row", "col"), None),
    )
    out_specs = P(("scen", "row", "col"), None)

    def per_device(border, panel_border, kinv, factor, root_block):
        schur, diag = gather(S, R, C, border, panel_border, kinv, factor, root_block)
        return finish(schur, diag)

    return jax.shard_map(
        per_device, mesh=mesh, in_specs=in_specs, out_specs=out_specs, check_vma=False
    )
```

```python
import functools

import jax
import jax.numpy as jnp
from jax import lax
from jax.experimental import pallas as pl
from jax.experimental.pallas import tpu as pltpu
from jax.sharding import PartitionSpec as P

MESH = pl.DeviceIdType.MESH
F32 = jnp.float32
BLOCK = 128
STRIP = 16
SLICES = 4
HIGHEST = lax.Precision.HIGHEST


def mm(a, b, da, db, precision=None):
    return lax.dot_general(
        a, b, (((da,), (db,)), ((), ())), precision=precision, preferred_element_type=F32
    )


def panel_kernel(
    S, R, C, slices,
    border_hbm, pb_hbm, kinv_hbm, factor_hbm, root_hbm, out_ref,
    border, pb, kinv, factor, root,
    lead, roots, solved, part, part_in, cp, rs_a, dp, rs_b, diag, upd, upd_in, rest, aug, work, inv,
    in_sem, top_send, top_recv, line_send, line_recv, p_send, p_recv,
    a_send, a_recv, b_send, b_recv, g_send, g_recv, h_send, h_recv,
    l_send, l_recv, u_send, u_recv,
):
    s, r, c = lax.axis_index("scen"), lax.axis_index("row"), lax.axis_index("col")
    rows, depth = factor.shape
    own, panel = root.shape
    wide = depth // slices
    half = panel // C
    n = half // S
    blocks = panel // BLOCK
    scenarios = kinv.shape[0]
    share = scenarios // C
    groups = cp.shape[0]

    def peer_s(o):
        return lax.rem(s + o, S)

    def fetch(k):
        src, dst = (
            (factor_hbm, factor), (root_hbm, root), (pb_hbm, pb), (kinv_hbm, kinv), (border_hbm, border)
        )[k]
        return pltpu.make_async_copy(src, dst, in_sem.at[k])

    for k in range(5):
        fetch(k).start()

    barrier = pltpu.get_barrier_semaphore()
    for o in range(1, S):
        pl.semaphore_signal(barrier, inc=1, device_id=(peer_s(o), r, c), device_id_type=MESH)
    for o in range(1, R):
        pl.semaphore_signal(barrier, inc=1, device_id=(s, lax.rem(r + o, R), c), device_id_type=MESH)
    pl.semaphore_signal(barrier, inc=1, device_id=(s, r, 1 - c), device_id_type=MESH)
    pl.semaphore_wait(barrier, S + R - 1)

    def remote(src, dst, send, recv, to):
        return pltpu.make_async_remote_copy(
            src_ref=src, dst_ref=dst, send_sem=send, recv_sem=recv, device_id=to, device_id_type=MESH
        )

    def mine_of(q):
        return pl.ds(pl.multiple_of(q * rows, rows), rows)

    def top_copy(j):
        return remote(
            factor_hbm.at[:, j * wide:(j + 1) * wide], lead.at[j, mine_of(r), :],
            top_send.at[j - 1], top_recv, (j, r, c),
        )

    def line_copy(kind, q, up):
        ref = roots.at[q] if kind else lead.at[jnp.minimum(s, slices - 1), mine_of(q), :]
        return remote(
            ref, ref, line_send.at[kind, q, 1 if up else 0], line_recv.at[kind, q],
            (s, lax.rem(r + (1 if up else R - 1), R), c),
        )

    def line_start(kind, q, up):
        @pl.when(r < R - 1 if up else r > 0)
        def _():
            line_copy(kind, q, up).start()

    def hop(kind, d):
        @pl.when(s < (1 if kind else slices))
        def _():
            @pl.when(r >= d)
            def _():
                line_copy(kind, r - d, True).wait_recv()
                line_start(kind, r - d, True)

            @pl.when(r + d < R)
            def _():
                line_copy(kind, r + d, False).wait_recv()
                line_start(kind, r + d, False)

    def line_sent(kind):
        @pl.when(s < (1 if kind else slices))
        def _():
            for d in range(R):
                @pl.when(jnp.logical_and(r < R - 1, r >= d))
                def _():
                    line_copy(kind, r - d, True).wait_send()

                @pl.when(jnp.logical_and(r > 0, r + d < R))
                def _():
                    line_copy(kind, r + d, False).wait_send()

    def block(o, core):
        return pl.ds(pl.multiple_of(core * half + peer_s(o) * n, n), n)

    def p_copy(o):
        at = block(o, 1 - c)
        return remote(part.at[at, :], part_in.at[o], p_send.at[o], p_recv.at[o], (s, r, 1 - c))

    def a_copy(o):
        return remote(
            cp.at[peer_s(o)], rs_a.at[o - 1], a_send.at[o - 1], a_recv.at[o - 1], (peer_s(o), r, c)
        )

    def b_copy(o):
        return remote(
            dp.at[o], rs_b.at[o - 1], b_send.at[o - 1], b_recv.at[o - 1], (peer_s(o), r, c)
        )

    def g_copy(o):
        ref = diag.at[block(0, c), :]
        return remote(ref, ref, g_send.at[o - 1], g_recv.at[o - 1], (peer_s(o), r, c))

    def h_copy(o):
        ref = diag.at[block(S - o if o else 0, c), :]
        return remote(ref, ref, h_send.at[o], h_recv.at[o], (s, r, 1 - c))

    def l_copy(o):
        ref = lead.at[jnp.minimum(s, slices - 1)]
        return remote(
            ref, ref, l_send.at[o - 1], l_recv.at[jnp.minimum(s, slices - 1)], (peer_s(o), r, c)
        )

    u_copy = remote(upd.at[1 - c], upd_in, u_send, u_recv, (s, r, 1 - c))

    @pl.when(s == 0)
    def _():
        for j in range(1, slices):
            top_copy(j).start()
    fetch(0).wait()
    fetch(1).wait()

    @pl.when(s == 0)
    def _():
        lead[0, mine_of(r), :] = factor[:, 0:wide]
        roots[r] = root[...]
        for up in (True, False):
            line_start(0, r, up)
            line_start(1, r, up)

    @pl.when(jnp.logical_and(s > 0, s < slices))
    def _():
        top_copy(1).wait_recv()
        for up in (True, False):
            line_start(0, r, up)

    def solve(i):
        sol = mm(kinv[i], pb[i], 1, 0).astype(jnp.bfloat16)
        solved[i] = sol
        return sol

    fetch(2).wait()
    fetch(3).wait()
    for k in range(share):
        i = c * share + k
        term = mm(pb[i], solve(i), 0, 0)
        if k == 0:
            part[...] = term
        else:
            part[...] += term
        if k + 1 < R:
            hop(0, k + 1)
            hop(1, k + 1)
    for d in range(share + 1, R):
        hop(0, d)
        hop(1, d)

    @pl.when(s == 0)
    def _():
        for q in range(R):
            at = pl.ds(pl.multiple_of((q * C + c) * own, own), own)
            part[at, :] += roots[q]

    def update_half(core):
        at = pl.ds(pl.multiple_of(core * half, half), half)

        @pl.when(s < slices)
        def _():
            slot = jnp.minimum(s, slices - 1)
            part[at, :] -= mm(lead[slot, at, :], lead[slot], 1, 1)

    update_half(1 - c)
    for o in range(S):
        p_copy(o).start()
    update_half(c)
    for o in list(range(1, S)) + [0]:
        p_copy(o).wait_recv()
        dp[o] = part[block(o, c), :] + part_in[o]
        if o:
            b_copy(o).start()

    fetch(4).wait()
    for k in range(scenarios - share):
        solve(lax.rem((c + 1) * share + k, scenarios))
    for g in range(groups):
        acc = mm(border[0, g], solved[0], 1, 0)
        for i in range(1, scenarios):
            acc += mm(border[i, g], solved[i], 1, 0)
        cp[g] = acc

    total = dp[0]
    for o in range(1, S):
        b_copy(o).wait_recv()
        total += rs_b[o - 1]
    diag[block(0, c), :] = total
    for o in range(1, S):
        g_copy(o).start()
    h_copy(0).start()
    for o in range(1, S):
        a_copy(o).start()

    @pl.when(s < slices)
    def _():
        for o in range(1, S):
            l_copy(o).start()

    for o in range(1, S):
        g_copy(o).wait_recv()
        h_copy(o).start()
    for o in range(S):
        h_copy(o).wait_recv()

    down = lax.broadcasted_iota(jnp.int32, (BLOCK, BLOCK), 0)
    across = lax.broadcasted_iota(jnp.int32, (BLOCK, BLOCK), 1)
    eye = jnp.where(down == across, 1.0, 0.0).astype(F32)
    aug[...] = diag[...].T

    @pl.loop(0, blocks)
    def _(J):
        @pl.when(J == blocks - 1)
        def _():
            for j in range(slices):
                @pl.when(s != j)
                def _():
                    remote(lead.at[j], lead.at[j], l_send.at[0], l_recv.at[j], (s, r, 1 - c)).wait_recv()
            product = mm(factor[:, 0:wide], lead[0], 1, 1)
            for j in range(1, slices):
                product += mm(factor[:, j * wide:(j + 1) * wide], lead[j], 1, 1)
            for q in range(C):
                upd[q] = product[q * own:(q + 1) * own]
            u_copy.start()
            acc = root[...] + cp[s]
            for o in range(1, S):
                a_copy(o).wait_recv()
                acc += rs_a[o - 1]
            rest[...] = acc

        at = pl.ds(pl.multiple_of(J * BLOCK, BLOCK), BLOCK)
        square = aug[at, at]
        work[:, 0:BLOCK] = jnp.where(down <= across, square, square.T)
        work[:, BLOCK:2 * BLOCK] = eye
        factor_block(work)
        inv[J] = work[:, BLOCK:2 * BLOCK]
        for j in range(blocks - 1):
            @pl.when(J == j)
            def _():
                lo, hi = j * BLOCK, (j + 1) * BLOCK
                across_rows = mm(inv[j], aug[lo:hi, hi:], 1, 0, HIGHEST)
                aug[lo:hi, hi:] = across_rows
                for i in range(j + 1, blocks):
                    at_i = (i - j - 1) * BLOCK
                    aug[i * BLOCK:(i + 1) * BLOCK, i * BLOCK:] -= mm(
                        across_rows[:, at_i:at_i + BLOCK], across_rows[:, at_i:], 0, 0, HIGHEST
                    )

    u_copy.wait()
    rest[...] -= upd[c] + upd_in[...]
    for j in range(blocks):
        lo, hi = j * BLOCK, (j + 1) * BLOCK
        solution_block = mm(rest[:, lo:hi], inv[j], 1, 1, HIGHEST)
        out_ref[:, lo:hi] = solution_block
        if hi < panel:
            rest[:, hi:] -= mm(solution_block, aug[lo:hi, hi:], 1, 0, HIGHEST)

    @pl.when(s == 0)
    def _():
        for j in range(1, slices):
            top_copy(j).wait_send()

    @pl.when(s < slices)
    def _():
        for o in range(1, S):
            l_copy(o).wait_send()

    line_sent(0)
    line_sent(1)
    for o in range(S):
        p_copy(o).wait_send()
        h_copy(o).wait_send()
    for o in range(1, S):
        a_copy(o).wait_send()
        b_copy(o).wait_send()
        g_copy(o).wait_send()


def panel_step(S, R, C, border, panel_border, kinv, factor, root):
    rows, depth = factor.shape
    own, panel = root.shape
    groups = border.shape[1]
    n = panel // C // S
    slices = min(S, SLICES)
    dma = pltpu.SemaphoreType.DMA
    bf16 = jnp.bfloat16
    vmem = pltpu.VMEM
    inputs = (border, panel_border, kinv, factor, root)
    return pl.pallas_call(
        functools.partial(panel_kernel, S, R, C, slices),
        out_shape=jax.ShapeDtypeStruct((own, panel), F32),
        in_specs=[pl.BlockSpec(memory_space=pl.ANY)] * len(inputs),
        out_specs=pl.BlockSpec(memory_space=pltpu.VMEM),
        scratch_shapes=[vmem(x.shape, x.dtype) for x in inputs] + [
            vmem((slices, R * rows, depth // slices), bf16),
            vmem((R, own, panel), F32),
            vmem(kinv.shape, bf16),
            vmem((panel, panel), F32),
            vmem((S, n, panel), F32),
            vmem((groups, own, panel), F32),
            vmem((S - 1, own, panel), F32),
            vmem((S, n, panel), F32),
            vmem((S - 1, n, panel), F32),
            vmem((panel, panel), F32),
            vmem((C, own, panel), F32),
            vmem((own, panel), F32),
            vmem((own, panel), F32),
            vmem((panel, panel), F32),
            vmem((BLOCK, 2 * BLOCK), F32),
            vmem((panel // BLOCK, BLOCK, BLOCK), F32),
            dma((len(inputs),)),
            dma((slices - 1,)), dma,
            dma((2, R, 2)), dma((2, R)),
            dma((S,)), dma((S,)),
            dma((S - 1,)), dma((S - 1,)),
            dma((S - 1,)), dma((S - 1,)),
            dma((S - 1,)), dma((S - 1,)),
            dma((S,)), dma((S,)),
            dma((S - 1,)), dma((slices,)),
            dma, dma,
        ],
        compiler_params=pltpu.CompilerParams(
            collective_id=0, has_side_effects=True, vmem_limit_bytes=56 * 1024 * 1024
        ),
    )(*inputs)


def factor_block(work):
    size = work.shape[0]
    sub = lax.broadcasted_iota(jnp.int32, (STRIP, BLOCK), 0)
    for j in range(size // STRIP):
        lo = j * STRIP
        left = work[lo:lo + STRIP, 0:BLOCK]
        right = work[lo:lo + STRIP, BLOCK:2 * BLOCK]
        cols = [
            jnp.broadcast_to(left[:, lo + b:lo + b + 1], (STRIP, BLOCK)) for b in range(STRIP)
        ]
        scale = jnp.zeros((STRIP, BLOCK), F32)
        for k in range(STRIP):
            pivot = jnp.broadcast_to(cols[k][k:k + 1, :], (STRIP, BLOCK))
            inverse = pl.reciprocal(pivot, approx=True)
            inverse = inverse * (2.0 - pivot * inverse)
            scale = jnp.where(sub == k, lax.rsqrt(pivot), scale)
            if k + 1 < STRIP:
                times = jnp.where(sub > k, cols[k] * inverse, 0.0)
                for b in range(k + 1, STRIP):
                    cols[b] = cols[b] - times * cols[b][k:k + 1, :]
                left = left - times * left[k:k + 1, :]
                right = right - times * right[k:k + 1, :]
        left = left * scale
        right = right * scale
        work[lo:lo + STRIP, 0:BLOCK] = left
        work[lo:lo + STRIP, BLOCK:2 * BLOCK] = right
        if lo + STRIP < size:
            both = jnp.concatenate([left, right], axis=1)
            work[lo + STRIP:, :] -= mm(left, both, 0, 0, HIGHEST)[lo + STRIP:, :]


def solution(mesh):
    S, R, C = mesh.shape["scen"], mesh.shape["row"], mesh.shape["col"]
    in_specs = (
        P("scen", None, ("row", "col"), None),
        P("scen", None, None),
        P("scen", None, None),
        P(("scen", "row"), "col"),
        P(("scen", "row", "col"), None),
    )
    out_specs = P(("scen", "row", "col"), None)

    def per_device(border, panel_border, kinv, factor, root_block):
        return panel_step(S, R, C, border, panel_border, kinv, factor, root_block)

    return jax.shard_map(
        per_device, mesh=mesh, in_specs=in_specs, out_specs=out_specs, check_vma=False
    )
```

```python
import functools

import jax
import jax.numpy as jnp
from jax import lax
from jax.experimental import pallas as pl
from jax.experimental.pallas import tpu as pltpu
from jax.sharding import PartitionSpec as P

MESH = pl.DeviceIdType.MESH
F32 = jnp.float32
BLOCK = 128
STRIP = 16
SLICES = 4


def mm(a, b, da, db):
    return lax.dot_general(a, b, (((da,), (db,)), ((), ())), preferred_element_type=F32)


def split(x):
    high = x.astype(jnp.bfloat16)
    left = x - high.astype(F32)
    middle = left.astype(jnp.bfloat16)
    return high, middle, (left - middle.astype(F32)).astype(jnp.bfloat16)


def mm_f32(a, b, da, db):
    ah, am, al = split(a)
    bh, bm, bl = split(b)
    return mm(
        jnp.concatenate([al, am, ah, am, ah, ah], axis=da),
        jnp.concatenate([bh, bm, bl, bh, bm, bh], axis=db),
        da, db,
    )


def panel_kernel(
    S, R, C, slices,
    border_hbm, pb_hbm, kinv_hbm, factor_hbm, root_hbm, out_ref,
    border, pb, kinv, factor, root,
    lead, roots, solved, part, part_in, cp, rs_a, dp, rs_b, diag, columns, upd, upd_in, rest, aug, work, inv,
    in_sem, f_send, f_recv, line_send, line_recv, p_send, p_recv,
    a_send, a_recv, b_send, b_recv, g_send, g_recv, h_send, h_recv,
    u_send, u_recv,
):
    s, r, c = lax.axis_index("scen"), lax.axis_index("row"), lax.axis_index("col")
    rows, depth = factor.shape
    own, panel = root.shape
    wide = depth // slices
    half = panel // C
    n = half // S
    blocks = panel // BLOCK
    scenarios = kinv.shape[0]
    share = scenarios // C
    groups = cp.shape[0]

    def peer_s(o):
        return lax.rem(s + o, S)

    def fetch(k):
        src, dst = (
            (factor_hbm, factor), (root_hbm, root), (pb_hbm, pb), (kinv_hbm, kinv), (border_hbm, border)
        )[k]
        return pltpu.make_async_copy(src, dst, in_sem.at[k])

    for k in range(5):
        fetch(k).start()

    barrier = pltpu.get_barrier_semaphore()
    for o in range(1, S):
        pl.semaphore_signal(barrier, inc=1, device_id=(peer_s(o), r, c), device_id_type=MESH)
    for o in range(1, R):
        pl.semaphore_signal(barrier, inc=1, device_id=(s, lax.rem(r + o, R), c), device_id_type=MESH)
    pl.semaphore_signal(barrier, inc=1, device_id=(s, r, 1 - c), device_id_type=MESH)
    pl.semaphore_wait(barrier, S + R - 1)

    def remote(src, dst, send, recv, to):
        return pltpu.make_async_remote_copy(
            src_ref=src, dst_ref=dst, send_sem=send, recv_sem=recv, device_id=to, device_id_type=MESH
        )

    def mine_of(q):
        return pl.ds(pl.multiple_of(q * rows, rows), rows)

    def f_copy(j):
        return remote(
            factor_hbm.at[:, j * wide:(j + 1) * wide], columns.at[s], f_send.at[j], f_recv.at[s],
            (j, r, c),
        )

    def f_start():
        for j in range(slices):
            @pl.when(s != j)
            def _():
                f_copy(j).start()

    def f_arrived(q):
        remote(columns.at[q], columns.at[q], f_send.at[0], f_recv.at[q], (s, r, 1 - c)).wait_recv()

    def line_copy(kind, q, up):
        ref = roots.at[q] if kind else lead.at[mine_of(q), :]
        return remote(
            ref, ref, line_send.at[kind, q, 1 if up else 0], line_recv.at[kind, q],
            (s, lax.rem(r + (1 if up else R - 1), R), c),
        )

    def line_start(kind, q, up):
        @pl.when(r < R - 1 if up else r > 0)
        def _():
            line_copy(kind, q, up).start()

    def hop(kind, d):
        @pl.when(s < (1 if kind else slices))
        def _():
            @pl.when(r >= d)
            def _():
                line_copy(kind, r - d, True).wait_recv()
                line_start(kind, r - d, True)

            @pl.when(r + d < R)
            def _():
                line_copy(kind, r + d, False).wait_recv()
                line_start(kind, r + d, False)

    def line_sent(kind):
        @pl.when(s < (1 if kind else slices))
        def _():
            for d in range(R):
                @pl.when(jnp.logical_and(r < R - 1, r >= d))
                def _():
                    line_copy(kind, r - d, True).wait_send()

                @pl.when(jnp.logical_and(r > 0, r + d < R))
                def _():
                    line_copy(kind, r + d, False).wait_send()

    def block(o, core):
        return pl.ds(pl.multiple_of(core * half + peer_s(o) * n, n), n)

    def p_copy(o):
        at = block(o, 1 - c)
        return remote(part.at[at, :], part_in.at[o], p_send.at[o], p_recv.at[o], (s, r, 1 - c))

    def a_copy(o):
        return remote(
            cp.at[peer_s(o)], rs_a.at[o - 1], a_send.at[o - 1], a_recv.at[o - 1], (peer_s(o), r, c)
        )

    def b_copy(o):
        return remote(
            dp.at[o], rs_b.at[o - 1], b_send.at[o - 1], b_recv.at[o - 1], (peer_s(o), r, c)
        )

    def g_copy(o):
        ref = diag.at[block(0, c), :]
        return remote(ref, ref, g_send.at[o - 1], g_recv.at[o - 1], (peer_s(o), r, c))

    def h_copy(o):
        ref = diag.at[block(S - o if o else 0, c), :]
        return remote(ref, ref, h_send.at[o], h_recv.at[o], (s, r, 1 - c))

    def u_copy():
        return remote(upd.at[1 - c], upd_in, u_send, u_recv, (s, r, 1 - c))

    @pl.when(s == 0)
    def _():
        f_start()
    fetch(0).wait()
    fetch(1).wait()
    for j in range(slices):
        @pl.when(s == j)
        def _():
            columns[j] = factor[:, j * wide:(j + 1) * wide]

    @pl.when(s == 0)
    def _():
        roots[r] = root[...]
        for up in (True, False):
            line_start(1, r, up)

    @pl.when(s < slices)
    def _():
        @pl.when(s != 0)
        def _():
            f_arrived(0)

        lead[mine_of(r), :] = columns[0]
        for up in (True, False):
            line_start(0, r, up)

    @pl.when(s != 0)
    def _():
        f_start()

    def solve(i):
        sol = mm(kinv[i], pb[i], 1, 0).astype(jnp.bfloat16)
        solved[i] = sol
        return sol

    fetch(2).wait()
    fetch(3).wait()
    for k in range(share):
        i = c * share + k
        term = mm(pb[i], solve(i), 0, 0)
        if k == 0:
            part[...] = term
        else:
            part[...] += term
        if k + 1 < R:
            hop(0, k + 1)
            hop(1, k + 1)
    for d in range(share + 1, R):
        hop(0, d)
        hop(1, d)

    @pl.when(s == 0)
    def _():
        for q in range(R):
            at = pl.ds(pl.multiple_of((q * C + c) * own, own), own)
            part[at, :] += roots[q]

    def update_half(core):
        at = pl.ds(pl.multiple_of(core * half, half), half)

        @pl.when(s < slices)
        def _():
            part[at, :] -= mm(lead[at, :], lead[...], 1, 1)

    update_half(1 - c)
    for o in range(S):
        p_copy(o).start()
    update_half(c)
    for o in list(range(1, S)) + [0]:
        p_copy(o).wait_recv()
        dp[o] = part[block(o, c), :] + part_in[o]
        if o:
            b_copy(o).start()

    fetch(4).wait()
    for k in range(scenarios - share):
        solve(lax.rem((c + 1) * share + k, scenarios))
    for g in range(groups):
        acc = mm(border[0, g], solved[0], 1, 0)
        for i in range(1, scenarios):
            acc += mm(border[i, g], solved[i], 1, 0)
        cp[g] = acc

    @pl.when(s < slices)
    def _():
        for q in range(S):
            @pl.when(s != q)
            def _():
                if q:
                    f_arrived(q)

            term = mm(columns[q], lead[...], 1, 1)
            for k in range(C):
                upd[k, q] = term[k * own:(k + 1) * own]
        u_copy().start()

    total = dp[0]
    for o in range(1, S):
        b_copy(o).wait_recv()
        total += rs_b[o - 1]
    diag[block(0, c), :] = total
    for o in range(1, S):
        g_copy(o).start()
    h_copy(0).start()

    @pl.when(s < slices)
    def _():
        u_copy().wait()
        for q in range(S):
            cp[q] -= upd[c, q] + upd_in[q]

    for o in range(1, S):
        a_copy(o).start()
    for o in range(1, S):
        g_copy(o).wait_recv()
        h_copy(o).start()
    for o in range(S):
        h_copy(o).wait_recv()

    down = lax.broadcasted_iota(jnp.int32, (BLOCK, BLOCK), 0)
    across = lax.broadcasted_iota(jnp.int32, (BLOCK, BLOCK), 1)
    eye = jnp.where(down == across, 1.0, 0.0).astype(F32)
    aug[...] = diag[...].T

    @pl.loop(0, blocks)
    def _(J):
        at = pl.ds(pl.multiple_of(J * BLOCK, BLOCK), BLOCK)
        square = aug[at, at]
        work[:, 0:BLOCK] = jnp.where(down <= across, square, square.T)
        work[:, BLOCK:2 * BLOCK] = eye
        factor_block(work)
        inv[J] = work[:, BLOCK:2 * BLOCK]
        for j in range(blocks - 1):
            @pl.when(J == j)
            def _():
                lo, hi = j * BLOCK, (j + 1) * BLOCK
                across_rows = mm_f32(inv[j], aug[lo:hi, hi:], 1, 0)
                aug[lo:hi, hi:] = across_rows
                for i in range(j + 1, blocks):
                    at_i = (i - j - 1) * BLOCK
                    aug[i * BLOCK:(i + 1) * BLOCK, i * BLOCK:] -= mm_f32(
                        across_rows[:, at_i:at_i + BLOCK], across_rows[:, at_i:], 0, 0
                    )

    acc = root[...] + cp[s]
    for o in range(1, S):
        a_copy(o).wait_recv()
        acc += rs_a[o - 1]
    rest[...] = acc
    for j in range(blocks):
        lo, hi = j * BLOCK, (j + 1) * BLOCK
        solution_block = mm_f32(rest[:, lo:hi], inv[j], 1, 1)
        out_ref[:, lo:hi] = solution_block
        if hi < panel:
            rest[:, hi:] -= mm_f32(solution_block, aug[lo:hi, hi:], 1, 0)

    for j in range(slices):
        @pl.when(s != j)
        def _():
            f_copy(j).wait_send()

    line_sent(0)
    line_sent(1)
    for o in range(S):
        p_copy(o).wait_send()
        h_copy(o).wait_send()
    for o in range(1, S):
        a_copy(o).wait_send()
        b_copy(o).wait_send()
        g_copy(o).wait_send()


def panel_step(S, R, C, border, panel_border, kinv, factor, root):
    rows, depth = factor.shape
    own, panel = root.shape
    groups = border.shape[1]
    n = panel // C // S
    slices = min(S, SLICES)
    dma = pltpu.SemaphoreType.DMA
    bf16 = jnp.bfloat16
    vmem = pltpu.VMEM
    inputs = (border, panel_border, kinv, factor, root)
    return pl.pallas_call(
        functools.partial(panel_kernel, S, R, C, slices),
        out_shape=jax.ShapeDtypeStruct((own, panel), F32),
        in_specs=[pl.BlockSpec(memory_space=pl.ANY)] * len(inputs),
        out_specs=pl.BlockSpec(memory_space=pltpu.VMEM),
        scratch_shapes=[vmem(x.shape, x.dtype) for x in inputs] + [
            vmem((R * rows, depth // slices), bf16),
            vmem((R, own, panel), F32),
            vmem(kinv.shape, bf16),
            vmem((panel, panel), F32),
            vmem((S, n, panel), F32),
            vmem((groups, own, panel), F32),
            vmem((S - 1, own, panel), F32),
            vmem((S, n, panel), F32),
            vmem((S - 1, n, panel), F32),
            vmem((panel, panel), F32),
            vmem((S, rows, depth // slices), bf16),
            vmem((C, S, own, panel), F32),
            vmem((S, own, panel), F32),
            vmem((own, panel), F32),
            vmem((panel, panel), F32),
            vmem((BLOCK, 2 * BLOCK), F32),
            vmem((panel // BLOCK, BLOCK, BLOCK), F32),
            dma((len(inputs),)),
            dma((slices,)), dma((S,)),
            dma((2, R, 2)), dma((2, R)),
            dma((S,)), dma((S,)),
            dma((S - 1,)), dma((S - 1,)),
            dma((S - 1,)), dma((S - 1,)),
            dma((S - 1,)), dma((S - 1,)),
            dma((S,)), dma((S,)),
            dma, dma,
        ],
        compiler_params=pltpu.CompilerParams(
            collective_id=0, has_side_effects=True, vmem_limit_bytes=56 * 1024 * 1024
        ),
    )(*inputs)


def factor_block(work):
    size = work.shape[0]
    sub = lax.broadcasted_iota(jnp.int32, (STRIP, BLOCK), 0)
    for j in range(size // STRIP):
        lo = j * STRIP
        left = work[lo:lo + STRIP, 0:BLOCK]
        right = work[lo:lo + STRIP, BLOCK:2 * BLOCK]
        cols = [
            jnp.broadcast_to(left[:, lo + b:lo + b + 1], (STRIP, BLOCK)) for b in range(STRIP)
        ]
        scale = jnp.zeros((STRIP, BLOCK), F32)
        for k in range(STRIP):
            pivot = jnp.broadcast_to(cols[k][k:k + 1, :], (STRIP, BLOCK))
            inverse = pl.reciprocal(pivot, approx=True)
            inverse = inverse * (2.0 - pivot * inverse)
            scale = jnp.where(sub == k, lax.rsqrt(pivot), scale)
            if k + 1 < STRIP:
                times = jnp.where(sub > k, cols[k] * inverse, 0.0)
                for b in range(k + 1, STRIP):
                    cols[b] = cols[b] - times * cols[b][k:k + 1, :]
                left = left - times * left[k:k + 1, :]
                right = right - times * right[k:k + 1, :]
        left = left * scale
        right = right * scale
        work[lo:lo + STRIP, 0:BLOCK] = left
        work[lo:lo + STRIP, BLOCK:2 * BLOCK] = right
        if lo + STRIP < size:
            both = jnp.concatenate([left, right], axis=1)
            work[lo + STRIP:, :] -= mm_f32(left, both, 0, 0)[lo + STRIP:, :]


def solution(mesh):
    S, R, C = mesh.shape["scen"], mesh.shape["row"], mesh.shape["col"]
    in_specs = (
        P("scen", None, ("row", "col"), None),
        P("scen", None, None),
        P("scen", None, None),
        P(("scen", "row"), "col"),
        P(("scen", "row", "col"), None),
    )
    out_specs = P(("scen", "row", "col"), None)

    def per_device(border, panel_border, kinv, factor, root_block):
        return panel_step(S, R, C, border, panel_border, kinv, factor, root_block)

    return jax.shard_map(
        per_device, mesh=mesh, in_specs=in_specs, out_specs=out_specs, check_vma=False
    )
```

```python
import functools

import jax
import jax.numpy as jnp
from jax import lax
from jax.experimental import pallas as pl
from jax.experimental.pallas import tpu as pltpu
from jax.sharding import PartitionSpec as P

MESH = pl.DeviceIdType.MESH
F32 = jnp.float32
BLOCK = 128
STRIP = 16
SLICES = 4


def mm(a, b, da, db):
    return lax.dot_general(a, b, (((da,), (db,)), ((), ())), preferred_element_type=F32)


def split(x):
    high = x.astype(jnp.bfloat16)
    left = x - high.astype(F32)
    middle = left.astype(jnp.bfloat16)
    return high, middle, (left - middle.astype(F32)).astype(jnp.bfloat16)


def mm_f32(a, b, da, db):
    ah, am, al = split(a)
    bh, bm, bl = split(b)
    return mm(
        jnp.concatenate([al, am, ah, am, ah, ah], axis=da),
        jnp.concatenate([bh, bm, bl, bh, bm, bh], axis=db),
        da, db,
    )


def panel_kernel(
    S, R, C, slices,
    border_hbm, pb_hbm, kinv_hbm, factor_hbm, root_hbm, out_ref,
    border, pb, kinv, factor, root,
    lead, roots, solved, part, part_in, cp, rs_a, dp, rs_b, columns, upd, upd_in, rest, aug, work, inv,
    in_sem, f_send, f_recv, line_send, line_recv, p_send, p_recv,
    a_send, a_recv, b_send, b_recv, g_send, g_recv,
    u_send, u_recv,
):
    s, r, c = lax.axis_index("scen"), lax.axis_index("row"), lax.axis_index("col")
    rows, depth = factor.shape
    own, panel = root.shape
    wide = depth // slices
    blocks = panel // BLOCK
    scenarios = kinv.shape[0]
    share = scenarios // C
    groups = cp.shape[0]
    half = BLOCK // C
    n = rs_b.shape[2]
    owners = half // n
    parts = 2
    piece = rows // parts

    def peer_s(o):
        return lax.rem(s + o, S)

    def fetch(k):
        src, dst = (
            (factor_hbm, factor), (root_hbm, root), (pb_hbm, pb), (kinv_hbm, kinv), (border_hbm, border)
        )[k]
        return pltpu.make_async_copy(src, dst, in_sem.at[k])

    for k in range(5):
        fetch(k).start()

    barrier = pltpu.get_barrier_semaphore()
    for o in range(1, S):
        pl.semaphore_signal(barrier, inc=1, device_id=(peer_s(o), r, c), device_id_type=MESH)
        pl.semaphore_signal(barrier, inc=1, device_id=(peer_s(o), r, 1 - c), device_id_type=MESH)
    for o in range(1, R):
        pl.semaphore_signal(barrier, inc=1, device_id=(s, lax.rem(r + o, R), c), device_id_type=MESH)
    pl.semaphore_signal(barrier, inc=1, device_id=(s, r, 1 - c), device_id_type=MESH)
    pl.semaphore_wait(barrier, C * (S - 1) + R)

    def remote(src, dst, send, recv, to):
        return pltpu.make_async_remote_copy(
            src_ref=src, dst_ref=dst, send_sem=send, recv_sem=recv, device_id=to, device_id_type=MESH
        )

    def mine_of(q):
        return pl.ds(pl.multiple_of(q * rows, rows), rows)

    def f_copy(j):
        return remote(
            factor_hbm.at[:, j * wide:(j + 1) * wide], columns.at[s], f_send.at[j], f_recv.at[s],
            (j, r, c),
        )

    def f_start():
        for j in range(slices):
            @pl.when(s != j)
            def _():
                f_copy(j).start()

    def f_arrived(q):
        remote(columns.at[q], columns.at[q], f_send.at[0], f_recv.at[q], (s, r, 1 - c)).wait_recv()

    def line_copy(kind, q, up):
        if kind == parts:
            ref = roots.at[q]
        else:
            ref = lead.at[pl.ds(pl.multiple_of(q * rows + kind * piece, piece), piece), :]
        return remote(
            ref, ref, line_send.at[kind, q, 1 if up else 0], line_recv.at[kind, q],
            (s, lax.rem(r + (1 if up else R - 1), R), c),
        )

    def line_start(kind, q, up):
        @pl.when(r < R - 1 if up else r > 0)
        def _():
            line_copy(kind, q, up).start()

    def hop(kind, d):
        @pl.when(s < (1 if kind == parts else slices))
        def _():
            @pl.when(r >= d)
            def _():
                line_copy(kind, r - d, True).wait_recv()
                line_start(kind, r - d, True)

            @pl.when(r + d < R)
            def _():
                line_copy(kind, r + d, False).wait_recv()
                line_start(kind, r + d, False)

    def line_sent(kind):
        @pl.when(s < (1 if kind == parts else slices))
        def _():
            for d in range(R):
                @pl.when(jnp.logical_and(r < R - 1, r >= d))
                def _():
                    line_copy(kind, r - d, True).wait_send()

                @pl.when(jnp.logical_and(r > 0, r + d < R))
                def _():
                    line_copy(kind, r + d, False).wait_send()

    def p_copy(J):
        at = pl.ds(pl.multiple_of(J * BLOCK + (1 - c) * half, half), half)
        return remote(
            part.at[at, J * BLOCK:], part_in.at[J, :, J * BLOCK:], p_send.at[J], p_recv.at[J],
            (s, r, 1 - c),
        )

    def a_copy(o):
        return remote(
            cp.at[peer_s(o)], rs_a.at[o - 1], a_send.at[o - 1], a_recv.at[o - 1], (peer_s(o), r, c)
        )

    def held(J, q, core):
        return pl.ds(pl.multiple_of(J * BLOCK + core * half + q * n, n), n)

    def b_copy(J, q):
        return remote(
            dp.at[J, q * n:(q + 1) * n, J * BLOCK:], rs_b.at[J, s, :, J * BLOCK:],
            b_send.at[J, q], b_recv.at[J, s], (q, r, c),
        )

    def b_start(J):
        for q in range(owners):
            @pl.when(s != q)
            def _():
                b_copy(J, q).start()

    def g_copy(J, o, turn):
        return remote(
            rs_b.at[J, s, :, J * BLOCK:], aug.at[held(J, s, c), J * BLOCK:], g_send.at[J, o, turn], g_recv.at[J, s, c],
            (peer_s(o), r, lax.rem(c + turn, C)),
        )

    targets = [(o, turn) for o in range(S) for turn in range(C) if o or turn]

    def b_sum(J):
        @pl.when(s < owners)
        def _():
            at = pl.ds(pl.multiple_of(s * n, n), n)
            total = dp[J, at, J * BLOCK:]
            for o in range(1, S):
                p = peer_s(o)
                ref = rs_b.at[J, p, :, J * BLOCK:]
                remote(ref, ref, b_send.at[J, 0], b_recv.at[J, p], (s, r, 1 - c)).wait_recv()
                total += rs_b[J, p, :, J * BLOCK:]
            aug[held(J, s, c), J * BLOCK:] = total
            rs_b[J, s, :, J * BLOCK:] = total
            for o, turn in targets:
                g_copy(J, o, turn).start()

    def g_arrived(J):
        for q in range(owners):
            for core in range(C):
                @pl.when(jnp.logical_or(s != q, c != core))
                def _():
                    ref = aug.at[held(J, q, core), J * BLOCK:]
                    remote(
                        ref, ref, g_send.at[J, 0, 1], g_recv.at[J, q, core], (s, r, 1 - c)
                    ).wait_recv()

    def u_copy():
        return remote(upd.at[1 - c], upd_in, u_send, u_recv, (s, r, 1 - c))

    @pl.when(s == 0)
    def _():
        f_start()
    fetch(0).wait()
    fetch(1).wait()
    for j in range(slices):
        @pl.when(s == j)
        def _():
            columns[j] = factor[:, j * wide:(j + 1) * wide]

    @pl.when(s == 0)
    def _():
        roots[r] = root[...]
        for up in (True, False):
            line_start(parts, r, up)

    @pl.when(s < slices)
    def _():
        @pl.when(s != 0)
        def _():
            f_arrived(0)

        lead[mine_of(r), :] = columns[0]
        for kind in range(parts):
            for up in (True, False):
                line_start(kind, r, up)

    @pl.when(s != 0)
    def _():
        f_start()

    def solve(i):
        sol = mm(kinv[i], pb[i], 1, 0).astype(jnp.bfloat16)
        solved[i] = sol
        return sol

    fetch(2).wait()
    fetch(3).wait()
    for k in range(share):
        i = c * share + k
        term = mm(solve(i), pb[i], 0, 0)
        if k == 0:
            part[...] = term
        else:
            part[...] += term

    def hops(d):
        for kind in range(parts + 1):
            hop(kind, d)

    def others():
        for k in range(scenarios - share):
            solve(lax.rem((c + 1) * share + k, scenarios))

    def couple():
        fetch(4).wait()
        for g in range(groups):
            acc = mm(border[0, g], solved[0], 1, 0)
            for i in range(1, scenarios):
                acc += mm(border[i, g], solved[i], 1, 0)
            cp[g] = acc

    between = {1: others, 2: couple}
    for d in range(1, max(R, 3)):
        if d < R:
            hops(d)
        if d in between:
            between[d]()

    @pl.when(s == 0)
    def _():
        for q in range(R):
            at = pl.ds(pl.multiple_of((q * C + c) * own, own), own)
            part[at, :] += roots[q]

    @pl.when(s < slices)
    def _():
        part[...] -= mm(lead[...], lead[...], 1, 1)

    for J in range(blocks):
        p_copy(J).start()
    for J in range(blocks):
        p_copy(J).wait_recv()
        at = pl.ds(pl.multiple_of(J * BLOCK + c * half, half), half)
        dp[J, :, J * BLOCK:] = part[at, J * BLOCK:] + part_in[J, :, J * BLOCK:]
        b_start(J)
    b_sum(0)

    @pl.when(s < slices)
    def _():
        for q in range(S):
            @pl.when(s != q)
            def _():
                if q:
                    f_arrived(q)

            term = mm(columns[q], lead[...], 1, 1)
            for k in range(C):
                upd[k, q] = term[k * own:(k + 1) * own]
        u_copy().start()

    for J in range(1, blocks):
        b_sum(J)

    @pl.when(s < slices)
    def _():
        u_copy().wait()
        for q in range(S):
            cp[q] -= upd[c, q] + upd_in[q]

    for o in range(1, S):
        a_copy(o).start()
    down = lax.broadcasted_iota(jnp.int32, (BLOCK, BLOCK), 0)
    across = lax.broadcasted_iota(jnp.int32, (BLOCK, BLOCK), 1)
    eye = jnp.where(down == across, 1.0, 0.0).astype(F32)

    @pl.loop(0, blocks)
    def _(J):
        for j in range(blocks):
            @pl.when(J == j)
            def _():
                g_arrived(j)
                lo, hi = j * BLOCK, (j + 1) * BLOCK
                if j:
                    aug[lo:hi, lo:] -= mm_f32(aug[0:lo, lo:hi], aug[0:lo, lo:], 0, 0)

        at = pl.ds(pl.multiple_of(J * BLOCK, BLOCK), BLOCK)
        square = aug[at, at]
        work[:, 0:BLOCK] = jnp.where(down <= across, square, square.T)
        work[:, BLOCK:2 * BLOCK] = eye
        factor_block(work)
        inv[J] = work[:, BLOCK:2 * BLOCK]
        for j in range(blocks - 1):
            @pl.when(J == j)
            def _():
                lo, hi = j * BLOCK, (j + 1) * BLOCK
                aug[lo:hi, hi:] = mm_f32(inv[j], aug[lo:hi, hi:], 1, 0)

    acc = root[...] + cp[s]
    for o in range(1, S):
        a_copy(o).wait_recv()
        acc += rs_a[o - 1]
    rest[...] = acc
    for j in range(blocks):
        lo, hi = j * BLOCK, (j + 1) * BLOCK
        solution_block = mm_f32(rest[:, lo:hi], inv[j], 1, 1)
        out_ref[:, lo:hi] = solution_block
        if hi < panel:
            rest[:, hi:] -= mm_f32(solution_block, aug[lo:hi, hi:], 1, 0)

    for j in range(slices):
        @pl.when(s != j)
        def _():
            f_copy(j).wait_send()

    for kind in range(parts + 1):
        line_sent(kind)
    for J in range(blocks):
        p_copy(J).wait_send()
        for q in range(owners):
            @pl.when(s != q)
            def _():
                b_copy(J, q).wait_send()

        @pl.when(s < owners)
        def _():
            for o, turn in targets:
                g_copy(J, o, turn).wait_send()

    for o in range(1, S):
        a_copy(o).wait_send()


def panel_step(S, R, C, border, panel_border, kinv, factor, root):
    rows, depth = factor.shape
    own, panel = root.shape
    groups = border.shape[1]
    blocks = panel // BLOCK
    half = BLOCK // C
    n = max(half // S, 8)
    slices = min(S, SLICES)
    dma = pltpu.SemaphoreType.DMA
    bf16 = jnp.bfloat16
    vmem = pltpu.VMEM
    inputs = (border, panel_border, kinv, factor, root)
    return pl.pallas_call(
        functools.partial(panel_kernel, S, R, C, slices),
        out_shape=jax.ShapeDtypeStruct((own, panel), F32),
        in_specs=[pl.BlockSpec(memory_space=pl.ANY)] * len(inputs),
        out_specs=pl.BlockSpec(memory_space=pltpu.VMEM),
        scratch_shapes=[vmem(x.shape, x.dtype) for x in inputs] + [
            vmem((R * rows, depth // slices), bf16),
            vmem((R, own, panel), F32),
            vmem(kinv.shape, bf16),
            vmem((panel, panel), F32),
            vmem((blocks, half, panel), F32),
            vmem((groups, own, panel), F32),
            vmem((S - 1, own, panel), F32),
            vmem((blocks, half, panel), F32),
            vmem((blocks, S, n, panel), F32),
            vmem((S, rows, depth // slices), bf16),
            vmem((C, S, own, panel), F32),
            vmem((S, own, panel), F32),
            vmem((own, panel), F32),
            vmem((panel, panel), F32),
            vmem((BLOCK, 2 * BLOCK), F32),
            vmem((panel // BLOCK, BLOCK, BLOCK), F32),
            dma((len(inputs),)),
            dma((slices,)), dma((S,)),
            dma((3, R, 2)), dma((3, R)),
            dma((blocks,)), dma((blocks,)),
            dma((S - 1,)), dma((S - 1,)),
            dma((blocks, S)), dma((blocks, S)),
            dma((blocks, S, C)), dma((blocks, S, C)),
            dma, dma,
        ],
        compiler_params=pltpu.CompilerParams(
            collective_id=0, has_side_effects=True, vmem_limit_bytes=56 * 1024 * 1024
        ),
    )(*inputs)


def factor_block(work):
    size = work.shape[0]
    sub = lax.broadcasted_iota(jnp.int32, (STRIP, BLOCK), 0)
    for j in range(size // STRIP):
        lo = j * STRIP
        left = work[lo:lo + STRIP, 0:BLOCK]
        right = work[lo:lo + STRIP, BLOCK:2 * BLOCK]
        cols = [
            jnp.broadcast_to(left[:, lo + b:lo + b + 1], (STRIP, BLOCK)) for b in range(STRIP)
        ]
        scale = jnp.zeros((STRIP, BLOCK), F32)
        for k in range(STRIP):
            pivot = jnp.broadcast_to(cols[k][k:k + 1, :], (STRIP, BLOCK))
            inverse = pl.reciprocal(pivot, approx=True)
            refine = 2.0 - pivot * inverse
            scale = jnp.where(sub == k, lax.rsqrt(pivot), scale)
            if k + 1 < STRIP:
                times = (jnp.where(sub > k, cols[k], 0.0) * inverse) * refine
                for b in range(k + 1, STRIP):
                    cols[b] = cols[b] - times * cols[b][k:k + 1, :]
                left = left - times * left[k:k + 1, :]
                right = right - times * right[k:k + 1, :]
        left = left * scale
        right = right * scale
        work[lo:lo + STRIP, 0:BLOCK] = left
        work[lo:lo + STRIP, BLOCK:2 * BLOCK] = right
        if lo + STRIP < size:
            both = jnp.concatenate([left, right], axis=1)
            work[lo + STRIP:, :] -= mm_f32(left, both, 0, 0)[lo + STRIP:, :]


def solution(mesh):
    S, R, C = mesh.shape["scen"], mesh.shape["row"], mesh.shape["col"]
    in_specs = (
        P("scen", None, ("row", "col"), None),
        P("scen", None, None),
        P("scen", None, None),
        P(("scen", "row"), "col"),
        P(("scen", "row", "col"), None),
    )
    out_specs = P(("scen", "row", "col"), None)

    def per_device(border, panel_border, kinv, factor, root_block):
        return panel_step(S, R, C, border, panel_border, kinv, factor, root_block)

    return jax.shard_map(
        per_device, mesh=mesh, in_specs=in_specs, out_specs=out_specs, check_vma=False
    )
```

```python
import functools

import jax
import jax.numpy as jnp
from jax import lax
from jax.experimental import pallas as pl
from jax.experimental.pallas import tpu as pltpu
from jax.sharding import PartitionSpec as P

MESH = pl.DeviceIdType.MESH
F32 = jnp.float32
BLOCK = 128
STRIP = 16
SLICES = 4


def mm(a, b, da, db):
    return lax.dot_general(a, b, (((da,), (db,)), ((), ())), preferred_element_type=F32)


def split(x):
    high = x.astype(jnp.bfloat16)
    left = x - high.astype(F32)
    middle = left.astype(jnp.bfloat16)
    return high, middle, (left - middle.astype(F32)).astype(jnp.bfloat16)


def mm_f32(a, b, da, db):
    ah, am, al = split(a)
    bh, bm, bl = split(b)
    return mm(
        jnp.concatenate([al, am, ah, am, ah, ah], axis=da),
        jnp.concatenate([bh, bm, bl, bh, bm, bh], axis=db),
        da, db,
    )


def panel_kernel(
    S, R, C, slices,
    border_hbm, pb_hbm, kinv_hbm, factor_hbm, root_hbm, out_ref,
    border, pb, kinv, factor, root,
    lead, roots, solved, part, part_in, cp, rs_a, dp, rs_b, columns, upd, upd_in, rest, aug, work, inv,
    in_sem, f_send, f_recv, line_send, line_recv, p_send, p_recv,
    a_send, a_recv, b_send, b_recv, g_send, g_recv,
    u_send, u_recv,
):
    s, r, c = lax.axis_index("scen"), lax.axis_index("row"), lax.axis_index("col")
    rows, depth = factor.shape
    own, panel = root.shape
    wide = depth // slices
    blocks = panel // BLOCK
    scenarios = kinv.shape[0]
    share = scenarios // C
    groups = cp.shape[0]
    half = BLOCK // C
    n = rs_b.shape[2]
    owners = half // n
    parts = 2
    piece = rows // parts

    def peer_s(o):
        return lax.rem(s + o, S)

    def fetch(k):
        src, dst = (
            (factor_hbm, factor), (root_hbm, root), (pb_hbm, pb), (kinv_hbm, kinv), (border_hbm, border)
        )[k]
        return pltpu.make_async_copy(src, dst, in_sem.at[k])

    for k in range(5):
        fetch(k).start()

    barrier = pltpu.get_barrier_semaphore()
    for o in range(1, S):
        pl.semaphore_signal(barrier, inc=1, device_id=(peer_s(o), r, c), device_id_type=MESH)
        pl.semaphore_signal(barrier, inc=1, device_id=(peer_s(o), r, 1 - c), device_id_type=MESH)
    for o in range(1, R):
        pl.semaphore_signal(barrier, inc=1, device_id=(s, lax.rem(r + o, R), c), device_id_type=MESH)
    pl.semaphore_signal(barrier, inc=1, device_id=(s, r, 1 - c), device_id_type=MESH)
    pl.semaphore_wait(barrier, C * (S - 1) + R)

    def remote(src, dst, send, recv, to):
        return pltpu.make_async_remote_copy(
            src_ref=src, dst_ref=dst, send_sem=send, recv_sem=recv, device_id=to, device_id_type=MESH
        )

    def mine_of(q):
        return pl.ds(pl.multiple_of(q * rows, rows), rows)

    def f_copy(j):
        return remote(
            factor_hbm.at[:, j * wide:(j + 1) * wide], columns.at[s], f_send.at[j], f_recv.at[s],
            (j, r, c),
        )

    def f_start():
        for j in range(slices):
            @pl.when(s != j)
            def _():
                f_copy(j).start()

    def f_arrived(q):
        remote(columns.at[q], columns.at[q], f_send.at[0], f_recv.at[q], (s, r, 1 - c)).wait_recv()

    def line_copy(kind, q, up):
        if kind == parts:
            ref = roots.at[q]
        else:
            ref = lead.at[pl.ds(pl.multiple_of(q * rows + kind * piece, piece), piece), :]
        return remote(
            ref, ref, line_send.at[kind, q, 1 if up else 0], line_recv.at[kind, q],
            (s, lax.rem(r + (1 if up else R - 1), R), c),
        )

    def line_start(kind, q, up):
        @pl.when(r < R - 1 if up else r > 0)
        def _():
            line_copy(kind, q, up).start()

    def hop(kind, d):
        @pl.when(s < (1 if kind == parts else slices))
        def _():
            @pl.when(r >= d)
            def _():
                line_copy(kind, r - d, True).wait_recv()
                line_start(kind, r - d, True)

            @pl.when(r + d < R)
            def _():
                line_copy(kind, r + d, False).wait_recv()
                line_start(kind, r + d, False)

    def line_sent(kind):
        @pl.when(s < (1 if kind == parts else slices))
        def _():
            for d in range(R):
                @pl.when(jnp.logical_and(r < R - 1, r >= d))
                def _():
                    line_copy(kind, r - d, True).wait_send()

                @pl.when(jnp.logical_and(r > 0, r + d < R))
                def _():
                    line_copy(kind, r + d, False).wait_send()

    def p_copy(J):
        at = pl.ds(pl.multiple_of(J * BLOCK + (1 - c) * half, half), half)
        return remote(
            part.at[at, J * BLOCK:], part_in.at[J, :, J * BLOCK:], p_send.at[J], p_recv.at[J],
            (s, r, 1 - c),
        )

    def a_copy(o):
        return remote(
            cp.at[peer_s(o)], rs_a.at[o - 1], a_send.at[o - 1], a_recv.at[o - 1], (peer_s(o), r, c)
        )

    def held(J, q, core):
        return pl.ds(pl.multiple_of(J * BLOCK + core * half + q * n, n), n)

    def b_copy(J, q):
        return remote(
            dp.at[J, q * n:(q + 1) * n, J * BLOCK:], rs_b.at[J, s, :, J * BLOCK:],
            b_send.at[J, q], b_recv.at[J, s], (q, r, c),
        )

    def b_start(J):
        for q in range(owners):
            @pl.when(s != q)
            def _():
                b_copy(J, q).start()

    def g_copy(J, o, turn):
        return remote(
            rs_b.at[J, s, :, J * BLOCK:], aug.at[held(J, s, c), J * BLOCK:], g_send.at[J, o, turn], g_recv.at[J, s, c],
            (peer_s(o), r, lax.rem(c + turn, C)),
        )

    targets = [(o, turn) for o in range(S) for turn in range(C) if o or turn]

    def b_sum(J):
        @pl.when(s < owners)
        def _():
            at = pl.ds(pl.multiple_of(s * n, n), n)
            total = dp[J, at, J * BLOCK:]
            for o in range(1, S):
                p = peer_s(o)
                ref = rs_b.at[J, p, :, J * BLOCK:]
                remote(ref, ref, b_send.at[J, 0], b_recv.at[J, p], (s, r, 1 - c)).wait_recv()
                total += rs_b[J, p, :, J * BLOCK:]
            aug[held(J, s, c), J * BLOCK:] = total
            rs_b[J, s, :, J * BLOCK:] = total
            for o, turn in targets:
                g_copy(J, o, turn).start()

    def g_arrived(J):
        for q in range(owners):
            for core in range(C):
                @pl.when(jnp.logical_or(s != q, c != core))
                def _():
                    ref = aug.at[held(J, q, core), J * BLOCK:]
                    remote(
                        ref, ref, g_send.at[J, 0, 1], g_recv.at[J, q, core], (s, r, 1 - c)
                    ).wait_recv()

    def u_copy():
        return remote(upd.at[1 - c], upd_in, u_send, u_recv, (s, r, 1 - c))

    @pl.when(s == 0)
    def _():
        f_start()
    fetch(0).wait()
    fetch(1).wait()
    for j in range(slices):
        @pl.when(s == j)
        def _():
            columns[j] = factor[:, j * wide:(j + 1) * wide]

    @pl.when(s == 0)
    def _():
        roots[r] = root[...]
        for up in (True, False):
            line_start(parts, r, up)

    @pl.when(s < slices)
    def _():
        @pl.when(s != 0)
        def _():
            f_arrived(0)

        lead[mine_of(r), :] = columns[0]
        for kind in range(parts):
            for up in (True, False):
                line_start(kind, r, up)

    @pl.when(s != 0)
    def _():
        f_start()

    def solve(i):
        sol = mm(kinv[i], pb[i], 1, 0).astype(jnp.bfloat16)
        solved[i] = sol
        return sol

    fetch(2).wait()
    fetch(3).wait()
    for k in range(share):
        i = c * share + k
        term = mm(solve(i), pb[i], 0, 0)
        if k == 0:
            part[...] = term
        else:
            part[...] += term

    def hops(d):
        for kind in range(parts + 1):
            hop(kind, d)

    def others():
        for k in range(scenarios - share):
            solve(lax.rem((c + 1) * share + k, scenarios))

    def couple():
        fetch(4).wait()
        for g in range(groups):
            acc = mm(border[0, g], solved[0], 1, 0)
            for i in range(1, scenarios):
                acc += mm(border[i, g], solved[i], 1, 0)
            cp[g] = acc

    between = {1: others, 2: couple}
    for d in range(1, max(R, 3)):
        if d < R:
            hops(d)
        if d in between:
            between[d]()

    @pl.when(s == 0)
    def _():
        for q in range(R):
            at = pl.ds(pl.multiple_of((q * C + c) * own, own), own)
            part[at, :] += roots[q]

    @pl.when(s < slices)
    def _():
        part[...] -= mm(lead[...], lead[...], 1, 1)

    for J in range(blocks):
        p_copy(J).start()
    for J in range(blocks):
        p_copy(J).wait_recv()
        at = pl.ds(pl.multiple_of(J * BLOCK + c * half, half), half)
        dp[J, :, J * BLOCK:] = part[at, J * BLOCK:] + part_in[J, :, J * BLOCK:]
        b_start(J)
    b_sum(0)

    @pl.when(s < slices)
    def _():
        for q in range(S):
            @pl.when(s != q)
            def _():
                if q:
                    f_arrived(q)

            term = mm(columns[q], lead[...], 1, 1)
            for k in range(C):
                upd[k, q] = term[k * own:(k + 1) * own]
        u_copy().start()

    for J in range(1, blocks):
        b_sum(J)

    @pl.when(s < slices)
    def _():
        u_copy().wait()
        for q in range(S):
            cp[q] -= upd[c, q] + upd_in[q]

    for o in range(1, S):
        a_copy(o).start()
    down = lax.broadcasted_iota(jnp.int32, (BLOCK, BLOCK), 0)
    across = lax.broadcasted_iota(jnp.int32, (BLOCK, BLOCK), 1)
    eye = jnp.where(down == across, 1.0, 0.0).astype(F32)

    @pl.loop(0, blocks)
    def _(J):
        for j in range(blocks):
            @pl.when(J == j)
            def _():
                g_arrived(j)
                lo, hi = j * BLOCK, (j + 1) * BLOCK
                if j:
                    aug[lo:hi, lo:] -= mm_f32(aug[0:lo, lo:hi], aug[0:lo, lo:], 0, 0)

        at = pl.ds(pl.multiple_of(J * BLOCK, BLOCK), BLOCK)
        square = aug[at, at]
        work[:, 0:BLOCK] = jnp.where(down <= across, square, square.T)
        work[:, BLOCK:2 * BLOCK] = eye
        factor_block(work)
        inv[J] = work[:, BLOCK:2 * BLOCK]
        for j in range(blocks - 1):
            @pl.when(J == j)
            def _():
                lo, hi = j * BLOCK, (j + 1) * BLOCK
                aug[lo:hi, hi:] = mm_f32(inv[j], aug[lo:hi, hi:], 1, 0)

    acc = root[...] + cp[s]
    for o in range(1, S):
        a_copy(o).wait_recv()
        acc += rs_a[o - 1]
    rest[...] = acc
    for j in range(blocks):
        lo, hi = j * BLOCK, (j + 1) * BLOCK
        solution_block = mm_f32(rest[:, lo:hi], inv[j], 1, 1)
        out_ref[:, lo:hi] = solution_block
        if hi < panel:
            rest[:, hi:] -= mm_f32(solution_block, aug[lo:hi, hi:], 1, 0)

    for j in range(slices):
        @pl.when(s != j)
        def _():
            f_copy(j).wait_send()

    for kind in range(parts + 1):
        line_sent(kind)
    for J in range(blocks):
        p_copy(J).wait_send()
        for q in range(owners):
            @pl.when(s != q)
            def _():
                b_copy(J, q).wait_send()

        @pl.when(s < owners)
        def _():
            for o, turn in targets:
                g_copy(J, o, turn).wait_send()

    for o in range(1, S):
        a_copy(o).wait_send()


def panel_step(S, R, C, border, panel_border, kinv, factor, root):
    rows, depth = factor.shape
    own, panel = root.shape
    groups = border.shape[1]
    blocks = panel // BLOCK
    half = BLOCK // C
    n = max(half // S, 8)
    slices = min(S, SLICES)
    dma = pltpu.SemaphoreType.DMA
    bf16 = jnp.bfloat16
    vmem = pltpu.VMEM
    inputs = (border, panel_border, kinv, factor, root)
    return pl.pallas_call(
        functools.partial(panel_kernel, S, R, C, slices),
        out_shape=jax.ShapeDtypeStruct((own, panel), F32),
        in_specs=[pl.BlockSpec(memory_space=pl.ANY)] * len(inputs),
        out_specs=pl.BlockSpec(memory_space=pltpu.VMEM),
        scratch_shapes=[vmem(x.shape, x.dtype) for x in inputs] + [
            vmem((R * rows, depth // slices), bf16),
            vmem((R, own, panel), F32),
            vmem(kinv.shape, bf16),
            vmem((panel, panel), F32),
            vmem((blocks, half, panel), F32),
            vmem((groups, own, panel), F32),
            vmem((S - 1, own, panel), F32),
            vmem((blocks, half, panel), F32),
            vmem((blocks, S, n, panel), F32),
            vmem((S, rows, depth // slices), bf16),
            vmem((C, S, own, panel), F32),
            vmem((S, own, panel), F32),
            vmem((own, panel), F32),
            vmem((panel, panel), F32),
            vmem((BLOCK, 2 * BLOCK), F32),
            vmem((panel // BLOCK, BLOCK, BLOCK), F32),
            dma((len(inputs),)),
            dma((slices,)), dma((S,)),
            dma((3, R, 2)), dma((3, R)),
            dma((blocks,)), dma((blocks,)),
            dma((S - 1,)), dma((S - 1,)),
            dma((blocks, S)), dma((blocks, S)),
            dma((blocks, S, C)), dma((blocks, S, C)),
            dma, dma,
        ],
        compiler_params=pltpu.CompilerParams(
            collective_id=0, has_side_effects=True, vmem_limit_bytes=56 * 1024 * 1024
        ),
    )(*inputs)


def factor_block(work):
    size = work.shape[0]
    sub = lax.broadcasted_iota(jnp.int32, (STRIP, BLOCK), 0)
    for j in range(size // STRIP):
        lo = j * STRIP
        left = work[lo:lo + STRIP, 0:BLOCK]
        right = work[lo:lo + STRIP, BLOCK:2 * BLOCK]
        cols = [
            jnp.broadcast_to(left[:, lo + b:lo + b + 1], (STRIP, BLOCK)) for b in range(STRIP)
        ]
        scale = jnp.zeros((STRIP, BLOCK), F32)
        for k in range(0, STRIP, 2):
            one, two = cols[k], cols[k + 1]
            a = jnp.broadcast_to(one[k:k + 1, :], (STRIP, BLOCK))
            b = jnp.broadcast_to(two[k:k + 1, :], (STRIP, BLOCK))
            d = jnp.broadcast_to(two[k + 1:k + 2, :], (STRIP, BLOCK))
            det = a * d - b * b
            inverse = pl.reciprocal(det, approx=True)
            refine = 2.0 - det * inverse
            first = pl.reciprocal(a, approx=True)
            first = first * (2.0 - a * first)
            scale = jnp.where(sub == k, lax.rsqrt(a), scale)
            scale = jnp.where(sub == k + 1, lax.rsqrt(det * first), scale)
            times = jnp.where(sub == k + 1, b * first, 0.0)
            if k + 2 < STRIP:
                times_one = (jnp.where(sub > k + 1, one * d - two * b, 0.0) * inverse) * refine
                times_two = (jnp.where(sub > k + 1, two * a - one * b, 0.0) * inverse) * refine
                for q in range(k + 2, STRIP):
                    cols[q] = cols[q] - (
                        times_one * cols[q][k:k + 1, :] + times_two * cols[q][k + 1:k + 2, :]
                    )
                times = times + times_one
                left, right = (
                    x - (times * x[k:k + 1, :] + times_two * x[k + 1:k + 2, :]) for x in (left, right)
                )
            else:
                left, right = (x - times * x[k:k + 1, :] for x in (left, right))
        left = left * scale
        right = right * scale
        work[lo:lo + STRIP, 0:BLOCK] = left
        work[lo:lo + STRIP, BLOCK:2 * BLOCK] = right
        if lo + STRIP < size:
            both = jnp.concatenate([left, right], axis=1)
            work[lo + STRIP:, :] -= mm_f32(left, both, 0, 0)[lo + STRIP:, :]


def solution(mesh):
    S, R, C = mesh.shape["scen"], mesh.shape["row"], mesh.shape["col"]
    in_specs = (
        P("scen", None, ("row", "col"), None),
        P("scen", None, None),
        P("scen", None, None),
        P(("scen", "row"), "col"),
        P(("scen", "row", "col"), None),
    )
    out_specs = P(("scen", "row", "col"), None)

    def per_device(border, panel_border, kinv, factor, root_block):
        return panel_step(S, R, C, border, panel_border, kinv, factor, root_block)

    return jax.shard_map(
        per_device, mesh=mesh, in_specs=in_specs, out_specs=out_specs, check_vma=False
    )
```

```python
import functools

import jax
import jax.numpy as jnp
from jax import lax
from jax.experimental import pallas as pl
from jax.experimental.pallas import tpu as pltpu
from jax.sharding import PartitionSpec as P

MESH = pl.DeviceIdType.MESH
F32 = jnp.float32
BLOCK = 128
STRIP = 16
SLICES = 4


def mm(a, b, da, db):
    return lax.dot_general(a, b, (((da,), (db,)), ((), ())), preferred_element_type=F32)


def split(x):
    high = x.astype(jnp.bfloat16)
    left = x - high.astype(F32)
    middle = left.astype(jnp.bfloat16)
    return high, middle, (left - middle.astype(F32)).astype(jnp.bfloat16)


def mm_f32(a, b, da, db):
    ah, am, al = split(a)
    bh, bm, bl = split(b)
    return mm(
        jnp.concatenate([al, am, ah, am, ah, ah], axis=da),
        jnp.concatenate([bh, bm, bl, bh, bm, bh], axis=db),
        da, db,
    )


def panel_kernel(
    S, R, C, slices,
    border_hbm, pb_hbm, kinv_hbm, factor_hbm, root_hbm, out_ref,
    border, pb, kinv, factor, root,
    lead, roots, solved, part, part_in, cp, rs_a, dp, rs_b, columns, upd, upd_in, rest, aug, work, inv,
    in_sem, f_send, f_recv, line_send, line_recv, p_send, p_recv,
    a_send, a_recv, b_send, b_recv, g_send, g_recv,
    u_send, u_recv,
):
    s, r, c = lax.axis_index("scen"), lax.axis_index("row"), lax.axis_index("col")
    rows, depth = factor.shape
    own, panel = root.shape
    wide = depth // slices
    blocks = panel // BLOCK
    scenarios = kinv.shape[0]
    share = scenarios // C
    groups = cp.shape[0]
    half = BLOCK // C
    n = rs_b.shape[2]
    owners = half // n
    parts = 2
    piece = rows // parts

    def peer_s(o):
        return lax.rem(s + o, S)

    def fetch(k):
        src, dst = (
            (factor_hbm, factor), (root_hbm, root), (pb_hbm, pb), (kinv_hbm, kinv), (border_hbm, border)
        )[k]
        return pltpu.make_async_copy(src, dst, in_sem.at[k])

    for k in range(5):
        fetch(k).start()

    barrier = pltpu.get_barrier_semaphore()
    for o in range(1, S):
        pl.semaphore_signal(barrier, inc=1, device_id=(peer_s(o), r, c), device_id_type=MESH)
        pl.semaphore_signal(barrier, inc=1, device_id=(peer_s(o), r, 1 - c), device_id_type=MESH)
    for o in range(1, R):
        pl.semaphore_signal(barrier, inc=1, device_id=(s, lax.rem(r + o, R), c), device_id_type=MESH)
    pl.semaphore_signal(barrier, inc=1, device_id=(s, r, 1 - c), device_id_type=MESH)
    pl.semaphore_wait(barrier, C * (S - 1) + R)

    def remote(src, dst, send, recv, to):
        return pltpu.make_async_remote_copy(
            src_ref=src, dst_ref=dst, send_sem=send, recv_sem=recv, device_id=to, device_id_type=MESH
        )

    def mine_of(q):
        return pl.ds(pl.multiple_of(q * rows, rows), rows)

    def f_copy(j):
        return remote(
            factor_hbm.at[:, j * wide:(j + 1) * wide], columns.at[s], f_send.at[j], f_recv.at[s],
            (j, r, c),
        )

    def f_start():
        for j in range(slices):
            @pl.when(s != j)
            def _():
                f_copy(j).start()

    def f_arrived(q):
        remote(columns.at[q], columns.at[q], f_send.at[0], f_recv.at[q], (s, r, 1 - c)).wait_recv()

    def line_copy(kind, q, up):
        if kind == parts:
            ref = roots.at[q]
        else:
            ref = lead.at[pl.ds(pl.multiple_of(q * rows + kind * piece, piece), piece), :]
        return remote(
            ref, ref, line_send.at[kind, q, 1 if up else 0], line_recv.at[kind, q],
            (s, lax.rem(r + (1 if up else R - 1), R), c),
        )

    def line_start(kind, q, up):
        @pl.when(r < R - 1 if up else r > 0)
        def _():
            line_copy(kind, q, up).start()

    def hop(kind, d):
        @pl.when(s < (1 if kind == parts else slices))
        def _():
            @pl.when(r >= d)
            def _():
                line_copy(kind, r - d, True).wait_recv()
                line_start(kind, r - d, True)

            @pl.when(r + d < R)
            def _():
                line_copy(kind, r + d, False).wait_recv()
                line_start(kind, r + d, False)

    def line_sent(kind):
        @pl.when(s < (1 if kind == parts else slices))
        def _():
            for d in range(R):
                @pl.when(jnp.logical_and(r < R - 1, r >= d))
                def _():
                    line_copy(kind, r - d, True).wait_send()

                @pl.when(jnp.logical_and(r > 0, r + d < R))
                def _():
                    line_copy(kind, r + d, False).wait_send()

    def p_copy(J):
        at = pl.ds(pl.multiple_of(J * BLOCK + (1 - c) * half, half), half)
        return remote(
            part.at[at, J * BLOCK:], part_in.at[J, :, J * BLOCK:], p_send.at[J], p_recv.at[J],
            (s, r, 1 - c),
        )

    def a_copy(o):
        return remote(
            cp.at[peer_s(o)], rs_a.at[o - 1], a_send.at[o - 1], a_recv.at[o - 1], (peer_s(o), r, c)
        )

    def held(J, q, core):
        return pl.ds(pl.multiple_of(J * BLOCK + core * half + q * n, n), n)

    def b_copy(J, q):
        return remote(
            dp.at[J, q * n:(q + 1) * n, J * BLOCK:], rs_b.at[J, s, :, J * BLOCK:],
            b_send.at[J, q], b_recv.at[J, s], (q, r, c),
        )

    def b_start(J):
        for q in range(owners):
            @pl.when(s != q)
            def _():
                b_copy(J, q).start()

    def g_copy(J, o, turn):
        return remote(
            rs_b.at[J, s, :, J * BLOCK:], aug.at[held(J, s, c), J * BLOCK:], g_send.at[J, o, turn], g_recv.at[J, s, c],
            (peer_s(o), r, lax.rem(c + turn, C)),
        )

    targets = [(o, turn) for o in range(S) for turn in range(C) if o or turn]

    def b_sum(J):
        @pl.when(s < owners)
        def _():
            at = pl.ds(pl.multiple_of(s * n, n), n)
            total = dp[J, at, J * BLOCK:]
            for o in range(1, S):
                p = peer_s(o)
                ref = rs_b.at[J, p, :, J * BLOCK:]
                remote(ref, ref, b_send.at[J, 0], b_recv.at[J, p], (s, r, 1 - c)).wait_recv()
                total += rs_b[J, p, :, J * BLOCK:]
            aug[held(J, s, c), J * BLOCK:] = total
            rs_b[J, s, :, J * BLOCK:] = total
            for o, turn in targets:
                g_copy(J, o, turn).start()

    def g_arrived(J):
        for q in range(owners):
            for core in range(C):
                @pl.when(jnp.logical_or(s != q, c != core))
                def _():
                    ref = aug.at[held(J, q, core), J * BLOCK:]
                    remote(
                        ref, ref, g_send.at[J, 0, 1], g_recv.at[J, q, core], (s, r, 1 - c)
                    ).wait_recv()

    def u_copy():
        return remote(upd.at[1 - c], upd_in, u_send, u_recv, (s, r, 1 - c))

    @pl.when(s == 0)
    def _():
        f_start()
    fetch(0).wait()
    fetch(1).wait()
    for j in range(slices):
        @pl.when(s == j)
        def _():
            columns[j] = factor[:, j * wide:(j + 1) * wide]

    @pl.when(s == 0)
    def _():
        roots[r] = root[...]
        for up in (True, False):
            line_start(parts, r, up)

    @pl.when(s < slices)
    def _():
        @pl.when(s != 0)
        def _():
            f_arrived(0)

        lead[mine_of(r), :] = columns[0]
        for kind in range(parts):
            for up in (True, False):
                line_start(kind, r, up)

    @pl.when(s != 0)
    def _():
        f_start()

    def solve(i):
        sol = mm(kinv[i], pb[i], 1, 0).astype(jnp.bfloat16)
        solved[i] = sol
        return sol

    fetch(2).wait()
    fetch(3).wait()
    for k in range(share):
        i = c * share + k
        term = mm(solve(i), pb[i], 0, 0)
        if k == 0:
            part[...] = term
        else:
            part[...] += term

    def hops(d):
        for kind in range(parts + 1):
            hop(kind, d)

    def others():
        for k in range(scenarios - share):
            solve(lax.rem((c + 1) * share + k, scenarios))

    def couple():
        fetch(4).wait()
        for g in range(groups):
            acc = mm(border[0, g], solved[0], 1, 0)
            for i in range(1, scenarios):
                acc += mm(border[i, g], solved[i], 1, 0)
            cp[g] = acc

    between = {1: others, 2: couple}
    for d in range(1, max(R, 3)):
        if d < R:
            hops(d)
        if d in between:
            between[d]()

    @pl.when(s == 0)
    def _():
        for q in range(R):
            at = pl.ds(pl.multiple_of((q * C + c) * own, own), own)
            part[at, :] += roots[q]

    @pl.when(s < slices)
    def _():
        part[...] -= mm(lead[...], lead[...], 1, 1)

    for J in range(blocks):
        p_copy(J).start()
    for J in range(blocks):
        p_copy(J).wait_recv()
        at = pl.ds(pl.multiple_of(J * BLOCK + c * half, half), half)
        dp[J, :, J * BLOCK:] = part[at, J * BLOCK:] + part_in[J, :, J * BLOCK:]
        b_start(J)
    b_sum(0)

    for J in range(1, blocks):
        b_sum(J)

    def update():
        @pl.when(s < slices)
        def _():
            for q in range(S):
                @pl.when(s != q)
                def _():
                    if q:
                        f_arrived(q)

                term = mm(columns[q], lead[...], 1, 1)
                for k in range(C):
                    upd[k, q] = term[k * own:(k + 1) * own]
            u_copy().start()

    def send_terms():
        @pl.when(s < slices)
        def _():
            u_copy().wait()
            for q in range(S):
                cp[q] -= upd[c, q] + upd_in[q]

        for o in range(1, S):
            a_copy(o).start()

    down = lax.broadcasted_iota(jnp.int32, (BLOCK, BLOCK), 0)
    across = lax.broadcasted_iota(jnp.int32, (BLOCK, BLOCK), 1)

    @pl.loop(0, blocks)
    def _(J):
        for j in range(blocks):
            @pl.when(J == j)
            def _():
                g_arrived(j)
                lo, hi = j * BLOCK, (j + 1) * BLOCK
                if j == min(1, blocks - 1):
                    update()
                if j == min(2, blocks - 1):
                    send_terms()
                if j:
                    aug[lo:hi, lo:] -= mm_f32(aug[0:lo, lo:hi], aug[0:lo, lo:], 0, 0)

        at = pl.ds(pl.multiple_of(J * BLOCK, BLOCK), BLOCK)
        square = aug[at, at]
        work[...] = jnp.where(down <= across, square, square.T)
        factor_block(work)
        inv[J] = jnp.where(down >= across, work[...], 0.0)
        for j in range(blocks - 1):
            @pl.when(J == j)
            def _():
                lo, hi = j * BLOCK, (j + 1) * BLOCK
                aug[lo:hi, hi:] = mm_f32(inv[j], aug[lo:hi, hi:], 1, 0)

    acc = root[...] + cp[s]
    for o in range(1, S):
        a_copy(o).wait_recv()
        acc += rs_a[o - 1]
    rest[...] = acc
    for j in range(blocks):
        lo, hi = j * BLOCK, (j + 1) * BLOCK
        solution_block = mm_f32(rest[:, lo:hi], inv[j], 1, 1)
        out_ref[:, lo:hi] = solution_block
        if hi < panel:
            rest[:, hi:] -= mm_f32(solution_block, aug[lo:hi, hi:], 1, 0)

    for j in range(slices):
        @pl.when(s != j)
        def _():
            f_copy(j).wait_send()

    for kind in range(parts + 1):
        line_sent(kind)
    for J in range(blocks):
        p_copy(J).wait_send()
        for q in range(owners):
            @pl.when(s != q)
            def _():
                b_copy(J, q).wait_send()

        @pl.when(s < owners)
        def _():
            for o, turn in targets:
                g_copy(J, o, turn).wait_send()

    for o in range(1, S):
        a_copy(o).wait_send()


def panel_step(S, R, C, border, panel_border, kinv, factor, root):
    rows, depth = factor.shape
    own, panel = root.shape
    groups = border.shape[1]
    blocks = panel // BLOCK
    half = BLOCK // C
    n = max(half // S, 8)
    slices = min(S, SLICES)
    dma = pltpu.SemaphoreType.DMA
    bf16 = jnp.bfloat16
    vmem = pltpu.VMEM
    inputs = (border, panel_border, kinv, factor, root)
    return pl.pallas_call(
        functools.partial(panel_kernel, S, R, C, slices),
        out_shape=jax.ShapeDtypeStruct((own, panel), F32),
        in_specs=[pl.BlockSpec(memory_space=pl.ANY)] * len(inputs),
        out_specs=pl.BlockSpec(memory_space=pltpu.VMEM),
        scratch_shapes=[vmem(x.shape, x.dtype) for x in inputs] + [
            vmem((R * rows, depth // slices), bf16),
            vmem((R, own, panel), F32),
            vmem(kinv.shape, bf16),
            vmem((panel, panel), F32),
            vmem((blocks, half, panel), F32),
            vmem((groups, own, panel), F32),
            vmem((S - 1, own, panel), F32),
            vmem((blocks, half, panel), F32),
            vmem((blocks, S, n, panel), F32),
            vmem((S, rows, depth // slices), bf16),
            vmem((C, S, own, panel), F32),
            vmem((S, own, panel), F32),
            vmem((own, panel), F32),
            vmem((panel, panel), F32),
            vmem((BLOCK, BLOCK), F32),
            vmem((panel // BLOCK, BLOCK, BLOCK), F32),
            dma((len(inputs),)),
            dma((slices,)), dma((S,)),
            dma((3, R, 2)), dma((3, R)),
            dma((blocks,)), dma((blocks,)),
            dma((S - 1,)), dma((S - 1,)),
            dma((blocks, S)), dma((blocks, S)),
            dma((blocks, S, C)), dma((blocks, S, C)),
            dma, dma,
        ],
        compiler_params=pltpu.CompilerParams(
            collective_id=0, has_side_effects=True, vmem_limit_bytes=56 * 1024 * 1024
        ),
    )(*inputs)


def factor_block(work):
    size = work.shape[0]
    sub = lax.broadcasted_iota(jnp.int32, (STRIP, BLOCK), 0)
    lane = lax.broadcasted_iota(jnp.int32, (STRIP, BLOCK), 1)
    across = lax.broadcasted_iota(jnp.int32, (BLOCK, BLOCK), 1)
    for j in range(size // STRIP):
        lo = j * STRIP
        left = work[lo:lo + STRIP, :]
        cols = [
            jnp.broadcast_to(left[:, lo + b:lo + b + 1], (STRIP, BLOCK)) for b in range(STRIP)
        ]
        inside = jnp.logical_and(lane >= lo, lane < lo + STRIP)
        strip = jnp.where(lane - lo == sub, 1.0, jnp.where(inside, 0.0, left))
        scale = jnp.zeros((STRIP, BLOCK), F32)
        for k in range(0, STRIP, 2):
            one, two = cols[k], cols[k + 1]
            a = jnp.broadcast_to(one[k:k + 1, :], (STRIP, BLOCK))
            b = jnp.broadcast_to(two[k:k + 1, :], (STRIP, BLOCK))
            d = jnp.broadcast_to(two[k + 1:k + 2, :], (STRIP, BLOCK))
            det = a * d - b * b
            inverse = pl.reciprocal(det, approx=True)
            refine = 2.0 - det * inverse
            first = pl.reciprocal(a, approx=True)
            first = first * (2.0 - a * first)
            scale = jnp.where(sub == k, lax.rsqrt(a), scale)
            scale = jnp.where(sub == k + 1, lax.rsqrt(det * first), scale)
            times = jnp.where(sub == k + 1, b * first, 0.0)
            if k + 2 < STRIP:
                times_one = (jnp.where(sub > k + 1, one * d - two * b, 0.0) * inverse) * refine
                times_two = (jnp.where(sub > k + 1, two * a - one * b, 0.0) * inverse) * refine
                for q in range(k + 2, STRIP):
                    cols[q] = cols[q] - (
                        times_one * cols[q][k:k + 1, :] + times_two * cols[q][k + 1:k + 2, :]
                    )
                times = times + times_one
                strip = strip - (times * strip[k:k + 1, :] + times_two * strip[k + 1:k + 2, :])
            else:
                strip = strip - times * strip[k:k + 1, :]
        strip = strip * scale
        work[lo:lo + STRIP, :] = strip
        if lo + STRIP < size:
            below = work[lo + STRIP:, :]
            gone = jnp.logical_and(across[lo + STRIP:] >= lo, across[lo + STRIP:] < lo + STRIP)
            work[lo + STRIP:, :] = jnp.where(gone, 0.0, below) - mm_f32(strip, strip, 0, 0)[lo + STRIP:, :]


def solution(mesh):
    S, R, C = mesh.shape["scen"], mesh.shape["row"], mesh.shape["col"]
    in_specs = (
        P("scen", None, ("row", "col"), None),
        P("scen", None, None),
        P("scen", None, None),
        P(("scen", "row"), "col"),
        P(("scen", "row", "col"), None),
    )
    out_specs = P(("scen", "row", "col"), None)

    def per_device(border, panel_border, kinv, factor, root_block):
        return panel_step(S, R, C, border, panel_border, kinv, factor, root_block)

    return jax.shard_map(
        per_device, mesh=mesh, in_specs=in_specs, out_specs=out_specs, check_vma=False
    )
```

```python
import functools

import jax
import jax.numpy as jnp
from jax import lax
from jax.experimental import pallas as pl
from jax.experimental.pallas import tpu as pltpu
from jax.sharding import PartitionSpec as P

MESH = pl.DeviceIdType.MESH
F32 = jnp.float32
BLOCK = 128
STRIP = 16
SLICES = 4


def mm(a, b, da, db):
    return lax.dot_general(a, b, (((da,), (db,)), ((), ())), preferred_element_type=F32)


def split(x):
    high = x.astype(jnp.bfloat16)
    left = x - high.astype(F32)
    middle = left.astype(jnp.bfloat16)
    return high, middle, (left - middle.astype(F32)).astype(jnp.bfloat16)


def mm_f32(a, b, da, db):
    ah, am, al = split(a)
    bh, bm, bl = split(b)
    return mm(
        jnp.concatenate([al, am, ah, am, ah, ah], axis=da),
        jnp.concatenate([bh, bm, bl, bh, bm, bh], axis=db),
        da, db,
    )


def panel_kernel(
    S, R, C, slices,
    border_hbm, pb_hbm, kinv_hbm, factor_hbm, root_hbm, out_ref,
    border, pb, kinv, factor, root,
    lead, roots, solved, part, part_in, cp, rs_a, dp, rs_b, columns, upd, upd_in, rest, aug, work, inv,
    in_sem, f_send, f_recv, line_send, line_recv, p_send, p_recv,
    a_send, a_recv, b_send, b_recv, g_send, g_recv,
    u_send, u_recv,
):
    s, r, c = lax.axis_index("scen"), lax.axis_index("row"), lax.axis_index("col")
    rows, depth = factor.shape
    own, panel = root.shape
    wide = depth // slices
    blocks = panel // BLOCK
    scenarios = kinv.shape[0]
    share = scenarios // C
    groups = cp.shape[0]
    half = BLOCK // C
    n = rs_b.shape[2]
    owners = half // n
    parts = 2
    piece = rows // parts

    def peer_s(o):
        return lax.rem(s + o, S)

    def fetch(k):
        src, dst = (
            (factor_hbm, factor), (root_hbm, root), (pb_hbm, pb), (kinv_hbm, kinv), (border_hbm, border)
        )[k]
        return pltpu.make_async_copy(src, dst, in_sem.at[k])

    for k in range(5):
        fetch(k).start()

    barrier = pltpu.get_barrier_semaphore()
    for o in range(1, S):
        pl.semaphore_signal(barrier, inc=1, device_id=(peer_s(o), r, c), device_id_type=MESH)
        pl.semaphore_signal(barrier, inc=1, device_id=(peer_s(o), r, 1 - c), device_id_type=MESH)
    for o in range(1, R):
        pl.semaphore_signal(barrier, inc=1, device_id=(s, lax.rem(r + o, R), c), device_id_type=MESH)
    pl.semaphore_signal(barrier, inc=1, device_id=(s, r, 1 - c), device_id_type=MESH)
    pl.semaphore_wait(barrier, C * (S - 1) + R)

    def remote(src, dst, send, recv, to):
        return pltpu.make_async_remote_copy(
            src_ref=src, dst_ref=dst, send_sem=send, recv_sem=recv, device_id=to, device_id_type=MESH
        )

    def mine_of(q):
        return pl.ds(pl.multiple_of(q * rows, rows), rows)

    def f_copy(j):
        return remote(
            factor_hbm.at[:, j * wide:(j + 1) * wide], columns.at[s], f_send.at[j], f_recv.at[s],
            (j, r, c),
        )

    def f_start():
        for j in range(slices):
            @pl.when(s != j)
            def _():
                f_copy(j).start()

    def f_arrived(q):
        remote(columns.at[q], columns.at[q], f_send.at[0], f_recv.at[q], (s, r, 1 - c)).wait_recv()

    def line_copy(kind, q, up):
        if kind == parts:
            ref = roots.at[q]
        else:
            ref = lead.at[pl.ds(pl.multiple_of(q * rows + kind * piece, piece), piece), :]
        return remote(
            ref, ref, line_send.at[kind, q, 1 if up else 0], line_recv.at[kind, q],
            (s, lax.rem(r + (1 if up else R - 1), R), c),
        )

    def line_start(kind, q, up):
        @pl.when(r < R - 1 if up else r > 0)
        def _():
            line_copy(kind, q, up).start()

    def hop(kind, d):
        @pl.when(s < (1 if kind == parts else slices))
        def _():
            @pl.when(r >= d)
            def _():
                line_copy(kind, r - d, True).wait_recv()
                line_start(kind, r - d, True)

            @pl.when(r + d < R)
            def _():
                line_copy(kind, r + d, False).wait_recv()
                line_start(kind, r + d, False)

    def line_sent(kind):
        @pl.when(s < (1 if kind == parts else slices))
        def _():
            for d in range(R):
                @pl.when(jnp.logical_and(r < R - 1, r >= d))
                def _():
                    line_copy(kind, r - d, True).wait_send()

                @pl.when(jnp.logical_and(r > 0, r + d < R))
                def _():
                    line_copy(kind, r + d, False).wait_send()

    def p_copy(J):
        at = pl.ds(pl.multiple_of(J * BLOCK + (1 - c) * half, half), half)
        return remote(
            part.at[at, J * BLOCK:], part_in.at[J, :, J * BLOCK:], p_send.at[J], p_recv.at[J],
            (s, r, 1 - c),
        )

    def a_copy(o):
        return remote(
            cp.at[peer_s(o)], rs_a.at[o - 1], a_send.at[o - 1], a_recv.at[o - 1], (peer_s(o), r, c)
        )

    def held(J, q, core):
        return pl.ds(pl.multiple_of(J * BLOCK + core * half + q * n, n), n)

    def b_copy(J, q):
        return remote(
            dp.at[J, q * n:(q + 1) * n, J * BLOCK:], rs_b.at[J, s, :, J * BLOCK:],
            b_send.at[J, q], b_recv.at[J, s], (q, r, c),
        )

    def b_start(J):
        for q in range(owners):
            @pl.when(s != q)
            def _():
                b_copy(J, q).start()

    def g_copy(J, o, turn):
        return remote(
            rs_b.at[J, s, :, J * BLOCK:], aug.at[held(J, s, c), J * BLOCK:], g_send.at[J, o, turn], g_recv.at[J, s, c],
            (peer_s(o), r, lax.rem(c + turn, C)),
        )

    targets = [(o, turn) for o in range(S) for turn in range(C) if o or turn]

    def b_sum(J):
        @pl.when(s < owners)
        def _():
            at = pl.ds(pl.multiple_of(s * n, n), n)
            total = dp[J, at, J * BLOCK:]
            for o in range(1, S):
                p = peer_s(o)
                ref = rs_b.at[J, p, :, J * BLOCK:]
                remote(ref, ref, b_send.at[J, 0], b_recv.at[J, p], (s, r, 1 - c)).wait_recv()
                total += rs_b[J, p, :, J * BLOCK:]
            aug[held(J, s, c), J * BLOCK:] = total
            rs_b[J, s, :, J * BLOCK:] = total
            for o, turn in targets:
                g_copy(J, o, turn).start()

    def g_arrived(J):
        for q in range(owners):
            for core in range(C):
                @pl.when(jnp.logical_or(s != q, c != core))
                def _():
                    ref = aug.at[held(J, q, core), J * BLOCK:]
                    remote(
                        ref, ref, g_send.at[J, 0, 1], g_recv.at[J, q, core], (s, r, 1 - c)
                    ).wait_recv()

    def u_copy():
        return remote(upd.at[1 - c], upd_in, u_send, u_recv, (s, r, 1 - c))

    @pl.when(s == 0)
    def _():
        f_start()
    fetch(0).wait()
    fetch(1).wait()
    for j in range(slices):
        @pl.when(s == j)
        def _():
            columns[j] = factor[:, j * wide:(j + 1) * wide]

    @pl.when(s == 0)
    def _():
        roots[r] = root[...]
        for up in (True, False):
            line_start(parts, r, up)

    @pl.when(s < slices)
    def _():
        @pl.when(s != 0)
        def _():
            f_arrived(0)

        lead[mine_of(r), :] = columns[0]
        for kind in range(parts):
            for up in (True, False):
                line_start(kind, r, up)

    @pl.when(s != 0)
    def _():
        f_start()

    def solve(i):
        sol = mm(kinv[i], pb[i], 1, 0).astype(jnp.bfloat16)
        solved[i] = sol
        return sol

    fetch(2).wait()
    fetch(3).wait()
    for k in range(share):
        i = c * share + k
        term = mm(solve(i), pb[i], 0, 0)
        if k == 0:
            part[...] = term
        else:
            part[...] += term

    def hops(d):
        for kind in range(parts + 1):
            hop(kind, d)

    def others():
        for k in range(scenarios - share):
            solve(lax.rem((c + 1) * share + k, scenarios))

    def couple():
        fetch(4).wait()
        for g in range(groups):
            acc = mm(border[0, g], solved[0], 1, 0)
            for i in range(1, scenarios):
                acc += mm(border[i, g], solved[i], 1, 0)
            cp[g] = acc

    between = {1: others, 2: couple}
    for d in range(1, max(R, 3)):
        if d < R:
            hops(d)
        if d in between:
            between[d]()

    @pl.when(s == 0)
    def _():
        for q in range(R):
            at = pl.ds(pl.multiple_of((q * C + c) * own, own), own)
            part[at, :] += roots[q]

    @pl.when(s < slices)
    def _():
        part[...] -= mm(lead[...], lead[...], 1, 1)

    for J in range(blocks):
        p_copy(J).start()
    for J in range(blocks):
        p_copy(J).wait_recv()
        at = pl.ds(pl.multiple_of(J * BLOCK + c * half, half), half)
        dp[J, :, J * BLOCK:] = part[at, J * BLOCK:] + part_in[J, :, J * BLOCK:]
        b_start(J)
    b_sum(0)

    @pl.when(s < slices)
    def _():
        for q in range(S):
            @pl.when(s != q)
            def _():
                if q:
                    f_arrived(q)

            term = mm(columns[q], lead[...], 1, 1)
            for k in range(C):
                upd[k, q] = term[k * own:(k + 1) * own]
        u_copy().start()

    for J in range(1, blocks):
        b_sum(J)

    @pl.when(s < slices)
    def _():
        u_copy().wait()
        for q in range(S):
            cp[q] -= upd[c, q] + upd_in[q]

    for o in range(1, S):
        a_copy(o).start()
    down = lax.broadcasted_iota(jnp.int32, (BLOCK, BLOCK), 0)
    across = lax.broadcasted_iota(jnp.int32, (BLOCK, BLOCK), 1)

    @pl.loop(0, blocks)
    def _(J):
        for j in range(blocks):
            @pl.when(J == j)
            def _():
                g_arrived(j)
                lo, hi = j * BLOCK, (j + 1) * BLOCK
                if j:
                    aug[lo:hi, lo:] -= mm_f32(aug[0:lo, lo:hi], aug[0:lo, lo:], 0, 0)

        at = pl.ds(pl.multiple_of(J * BLOCK, BLOCK), BLOCK)
        square = aug[at, at]
        work[...] = jnp.where(down <= across, square, square.T)
        factor_block(work)
        inv[J] = jnp.where(down >= across, work[...], 0.0)
        for j in range(blocks - 1):
            @pl.when(J == j)
            def _():
                lo, hi = j * BLOCK, (j + 1) * BLOCK
                aug[lo:hi, hi:] = mm_f32(inv[j], aug[lo:hi, hi:], 1, 0)

    acc = root[...] + cp[s]
    for o in range(1, S):
        a_copy(o).wait_recv()
        acc += rs_a[o - 1]
    rest[...] = acc
    for j in range(blocks):
        lo, hi = j * BLOCK, (j + 1) * BLOCK
        solution_block = mm_f32(rest[:, lo:hi], inv[j], 1, 1)
        out_ref[:, lo:hi] = solution_block
        if hi < panel:
            rest[:, hi:] -= mm_f32(solution_block, aug[lo:hi, hi:], 1, 0)

    for j in range(slices):
        @pl.when(s != j)
        def _():
            f_copy(j).wait_send()

    for kind in range(parts + 1):
        line_sent(kind)
    for J in range(blocks):
        p_copy(J).wait_send()
        for q in range(owners):
            @pl.when(s != q)
            def _():
                b_copy(J, q).wait_send()

        @pl.when(s < owners)
        def _():
            for o, turn in targets:
                g_copy(J, o, turn).wait_send()

    for o in range(1, S):
        a_copy(o).wait_send()


def panel_step(S, R, C, border, panel_border, kinv, factor, root):
    rows, depth = factor.shape
    own, panel = root.shape
    groups = border.shape[1]
    blocks = panel // BLOCK
    half = BLOCK // C
    n = max(half // S, 8)
    slices = min(S, SLICES)
    dma = pltpu.SemaphoreType.DMA
    bf16 = jnp.bfloat16
    vmem = pltpu.VMEM
    inputs = (border, panel_border, kinv, factor, root)
    return pl.pallas_call(
        functools.partial(panel_kernel, S, R, C, slices),
        out_shape=jax.ShapeDtypeStruct((own, panel), F32),
        in_specs=[pl.BlockSpec(memory_space=pl.ANY)] * len(inputs),
        out_specs=pl.BlockSpec(memory_space=pltpu.VMEM),
        scratch_shapes=[vmem(x.shape, x.dtype) for x in inputs] + [
            vmem((R * rows, depth // slices), bf16),
            vmem((R, own, panel), F32),
            vmem(kinv.shape, bf16),
            vmem((panel, panel), F32),
            vmem((blocks, half, panel), F32),
            vmem((groups, own, panel), F32),
            vmem((S - 1, own, panel), F32),
            vmem((blocks, half, panel), F32),
            vmem((blocks, S, n, panel), F32),
            vmem((S, rows, depth // slices), bf16),
            vmem((C, S, own, panel), F32),
            vmem((S, own, panel), F32),
            vmem((own, panel), F32),
            vmem((panel, panel), F32),
            vmem((BLOCK, BLOCK), F32),
            vmem((panel // BLOCK, BLOCK, BLOCK), F32),
            dma((len(inputs),)),
            dma((slices,)), dma((S,)),
            dma((3, R, 2)), dma((3, R)),
            dma((blocks,)), dma((blocks,)),
            dma((S - 1,)), dma((S - 1,)),
            dma((blocks, S)), dma((blocks, S)),
            dma((blocks, S, C)), dma((blocks, S, C)),
            dma, dma,
        ],
        compiler_params=pltpu.CompilerParams(
            collective_id=0, has_side_effects=True, vmem_limit_bytes=56 * 1024 * 1024
        ),
    )(*inputs)


def factor_block(work):
    size = work.shape[0]
    sub = lax.broadcasted_iota(jnp.int32, (STRIP, BLOCK), 0)
    lane = lax.broadcasted_iota(jnp.int32, (STRIP, BLOCK), 1)
    across = lax.broadcasted_iota(jnp.int32, (BLOCK, BLOCK), 1)
    for j in range(size // STRIP):
        lo = j * STRIP
        left = work[lo:lo + STRIP, :]
        cols = [
            jnp.broadcast_to(left[:, lo + b:lo + b + 1], (STRIP, BLOCK)) for b in range(STRIP)
        ]
        inside = jnp.logical_and(lane >= lo, lane < lo + STRIP)
        strip = jnp.where(lane - lo == sub, 1.0, jnp.where(inside, 0.0, left))
        scale = jnp.zeros((STRIP, BLOCK), F32)
        for k in range(0, STRIP, 2):
            one, two = cols[k], cols[k + 1]
            a = jnp.broadcast_to(one[k:k + 1, :], (STRIP, BLOCK))
            b = jnp.broadcast_to(two[k:k + 1, :], (STRIP, BLOCK))
            d = jnp.broadcast_to(two[k + 1:k + 2, :], (STRIP, BLOCK))
            det = a * d - b * b
            inverse = pl.reciprocal(det, approx=True)
            refine = 2.0 - det * inverse
            first = pl.reciprocal(a, approx=True)
            first = first * (2.0 - a * first)
            scale = jnp.where(sub == k, lax.rsqrt(a), scale)
            scale = jnp.where(sub == k + 1, lax.rsqrt(det * first), scale)
            times = jnp.where(sub == k + 1, b * first, 0.0)
            if k + 2 < STRIP:
                times_one = (jnp.where(sub > k + 1, one * d - two * b, 0.0) * inverse) * refine
                times_two = (jnp.where(sub > k + 1, two * a - one * b, 0.0) * inverse) * refine
                for q in range(k + 2, STRIP):
                    cols[q] = cols[q] - (
                        times_one * cols[q][k:k + 1, :] + times_two * cols[q][k + 1:k + 2, :]
                    )
                times = times + times_one
                strip = strip - (times * strip[k:k + 1, :] + times_two * strip[k + 1:k + 2, :])
            else:
                strip = strip - times * strip[k:k + 1, :]
        strip = strip * scale
        work[lo:lo + STRIP, :] = strip
        if lo + STRIP < size:
            below = work[lo + STRIP:, :]
            gone = jnp.logical_and(across[lo + STRIP:] >= lo, across[lo + STRIP:] < lo + STRIP)
            work[lo + STRIP:, :] = jnp.where(gone, 0.0, below) - mm_f32(strip, strip, 0, 0)[lo + STRIP:, :]


def solution(mesh):
    S, R, C = mesh.shape["scen"], mesh.shape["row"], mesh.shape["col"]
    in_specs = (
        P("scen", None, ("row", "col"), None),
        P("scen", None, None),
        P("scen", None, None),
        P(("scen", "row"), "col"),
        P(("scen", "row", "col"), None),
    )
    out_specs = P(("scen", "row", "col"), None)

    def per_device(border, panel_border, kinv, factor, root_block):
        return panel_step(S, R, C, border, panel_border, kinv, factor, root_block)

    return jax.shard_map(
        per_device, mesh=mesh, in_specs=in_specs, out_specs=out_specs, check_vma=False
    )
```
